32 devices in a mesh: expert: 4 (over y, core), fsdp: 8 (over z, x).
Axes of the slice: x: 2, y: 2, z: 4, core: 2. Of those that a mesh axis runs over, the one named last changes fastest.
Arguments:
- tokens: bfloat16 [8192, 1536], P(('expert', 'fsdp')), may hold values from -6 to 6
- routes: int32 [8192, 4], P(('expert', 'fsdp')), may hold values from 0 to 31, all different within a row; in each aligned block of 256 rows (0 to 255, 256 to 511, ...) at most 48 rows name the same one
- norm_attn: float32 [1536], replicated, may hold values from 0.1 to 1.9
- qkv_weight: bfloat16 [1536, 2048], P('fsdp'), may hold values from -0.15625 to 0.15625
- out_weight: bfloat16 [1536, 1536], P('fsdp'), may hold values from -0.625 to 0.625
- norm_moe: float32 [1536], replicated, may hold values from 0.1 to 1.9
- router_weight: bfloat16 [1536, 32], replicated, may hold values from -0.078125 to 0.078125
- gate_up: bfloat16 [32, 1536, 1536], P('expert', 'fsdp'), may hold values from -0.15625 to 0.15625
- down: bfloat16 [32, 768, 1536], P('expert', 'fsdp'), may hold values from -0.625 to 0.625
- grad_output: bfloat16 [8192, 1536], P(('expert', 'fsdp')), may hold values from -6 to 6
Outputs:
- mixed: bfloat16 [8192, 1536], P(('expert', 'fsdp'))
- grad_tokens: float32 [8192, 1536], P(('expert', 'fsdp'))
- grad_norm_attn: float32 [1536], replicated
- grad_qkv: float32 [1536, 2048], P('fsdp')
- grad_out_proj: float32 [1536, 1536], P('fsdp')
- grad_norm_moe: float32 [1536], replicated
- grad_router: float32 [1536, 32], replicated
- grad_gate_up: float32 [32, 1536, 1536], P('expert', 'fsdp')
- grad_down: float32 [32, 768, 1536], P('expert', 'fsdp')
The draws below stay inside these ranges and needn't reach their ends.
Inputs may be any that keep to these rules, and one draw needn't show every extreme that they name: `routes`: each row names 4 different experts; in the 256 rows of one device no expert is named by more than 48 rows, and in every draw some device has an expert named by exactly 48 of its rows.
All inputs are finite; a program needn't handle non-finite values.
Results may differ from the reference program's by a relative error of at most 0.023.
Values may be sent and summed in bfloat16 or wider, within the bound.
No kernel may reach another device: no remote copies, remote signals or barrier semaphores. Data moves between devices by JAX's collectives and lax.ppermute only.
A program may use at most 320 MiB of HBM per device.

```python
import math
import jax
import jax.numpy as jnp
import numpy as np
from jax import lax

D = 1536
HEADS = 12
KV_HEADS = 2
HEAD_DIM = 128
FFE = 768
EXPERTS = 32
TOP = 4
TOK_DEV = 256
HQ = 1536
QKV = 2048
CAP = 48
TOKENS = 8192


def block_scale(own_key, shape, shards, low, high):
    def one(axis_at, parts):
        draws = jax.random.uniform(jax.random.fold_in(jax.random.fold_in(own_key, 6), axis_at), (parts,), jnp.float32, low / len(shards), high / len(shards))
        return jnp.repeat(jnp.exp(draws), shape[axis_at] // parts).reshape((-1,) + (1,) * (len(shape) - axis_at - 1))

    factor_of = one(*shards[0])
    for cut in shards[1:]:
        factor_of = factor_of * one(*cut)
    return factor_of


def deal_out(key, own, number, rows, amount, top, most, skew):
    order = jax.random.permutation(key, amount)
    crowded, common = load_shares(amount, rows * top, most, skew, True), load_shares(amount, rows * top, most, skew, False)
    places = jnp.arange(amount)

    def named(lengths, rotation):
        used = int((lengths > 0).sum())
        fixed = max(1, used // 4)
        moved = fixed + (places - fixed + rotation * (used - fixed)) % max(1, amount - fixed)
        return jnp.zeros((amount,), jnp.int32).at[order[jnp.where(places < fixed, places, moved)]].set(jnp.asarray(lengths, jnp.int32))

    lengths = jnp.where(number % 4 == 0, named(crowded, number // 4), named(common, number - number // 4 - 1))
    mixed = jax.random.permutation(jax.random.fold_in(own, 3), amount)
    source_of, receiver = mixed[0:amount // 2 * 2:2], mixed[1:amount // 2 * 2:2]
    room = jnp.minimum(lengths[source_of] - 1, most - lengths[receiver]) // 2
    room = jnp.where((source_of == order[0]) | (receiver == order[0]) | (lengths[receiver] == 0), 0, jnp.maximum(room, 0))
    moved = jax.random.randint(jax.random.fold_in(own, 4), (amount // 2,), 0, 1 << 20) % (room + 1)
    lengths = lengths.at[source_of].add(-moved).at[receiver].add(moved)
    items = jnp.searchsorted(jnp.cumsum(lengths), jnp.arange(rows * top), side="right").astype(jnp.int32)
    table = items.reshape(top, rows).T
    table = table[jax.random.permutation(jax.random.fold_in(own, 1), rows)]
    rotation = jax.random.randint(jax.random.fold_in(own, 2), (rows, 1), 0, top)
    return jnp.take_along_axis(table, (jnp.arange(top)[None, :] + rotation) % top, axis=1)


def load_shares(number_of, total, most, skew, full):
    portions = [(1 << 20) // math.isqrt(rank ** skew) + 1 for rank in range(1, number_of + 1)]
    largest = most if full else min(most, max(-(-total // number_of), total * portions[0] // sum(portions)))
    least = 1 if total - largest >= number_of - 1 else 0
    given, spare = [largest] + [least] * (number_of - 1), total - largest - least * (number_of - 1)
    while spare > 0:
        free = [i for i in range(1, number_of) if given[i] < largest] or [i for i in range(1, number_of) if given[i] < most]
        pool, remaining = sum([portions[i] for i in free]), spare
        for i in free:
            addition = min(most - given[i], max(1, remaining * portions[i] // pool), spare)
            given[i] = given[i] + addition
            spare = spare - addition
    return np.array(given)


def noise(stream_key, dims, scale, bound, shards=(), held_as=jnp.bfloat16):
    loudness = block_scale(stream_key, dims, shards, -0.22, 0.18) if shards else 1.0
    entries = jax.random.normal(stream_key, dims, jnp.float32) * scale * loudness
    return jnp.minimum(jnp.maximum(entries, -bound), bound).astype(held_as)


def setup_inputs(seed: int = 0) -> dict:
    streams_of = jax.random.split(jax.random.key(seed), 11)
    tokens = noise(streams_of[0], (TOKENS, D), 1.0, 6.0, ((0, 32),))
    routes_keys = jax.random.split(jax.random.fold_in(streams_of[1], 1), TOKENS // TOK_DEV)
    routes_turns = jax.random.permutation(jax.random.fold_in(streams_of[1], 3), TOKENS // TOK_DEV)
    routes = jax.vmap(lambda own, number: deal_out(jax.random.fold_in(streams_of[1], 2), own, number, TOK_DEV, EXPERTS, TOP, CAP, 1))(routes_keys, routes_turns).reshape((TOKENS, TOP))
    norm_attn = jnp.clip(1.0 + 0.18 * jax.random.normal(streams_of[2], (D,), jnp.float32), 0.1, 1.9)
    qkv_weight = noise(streams_of[3], (D, QKV), D ** -0.5, 0.15625, ((0, 8),))
    out_weight = noise(streams_of[4], (HQ, D), (HQ // 16) ** -0.5, 0.625, ((0, 8),))
    norm_moe = jnp.clip(1.0 + 0.18 * jax.random.normal(streams_of[5], (D,), jnp.float32), 0.1, 1.9)
    router_weight = noise(streams_of[6], (D, EXPERTS), (4 * D) ** -0.5, 0.078125)
    gate_up = noise(streams_of[7], (EXPERTS, D, 2 * FFE), D ** -0.5, 0.15625, ((0, 4), (1, 8)))
    down = noise(streams_of[8], (EXPERTS, FFE, D), (FFE // 8) ** -0.5, 0.625, ((0, 4), (1, 8)))
    grad_output = noise(streams_of[9], (TOKENS, D), 1.0, 6.0, ((0, 32),))
    return {"tokens": tokens, "routes": routes, "norm_attn": norm_attn, "qkv_weight": qkv_weight, "out_weight": out_weight, "norm_moe": norm_moe, "router_weight": router_weight, "gate_up": gate_up, "down": down, "grad_output": grad_output}


@jax.custom_vjp
def low(v):
    return lax.optimization_barrier(v.astype(jnp.bfloat16)).astype(jnp.float32)

@jax.custom_vjp
def low_back(v):
    return v

def low_keep(v):
    return (low(v), None)

def low_pass(kept, grad):
    return (grad,)

def back_keep(v):
    return (v, None)

def back_low(kept, grad):
    return (low(grad),)
low.defvjp(low_keep, low_pass)
low_back.defvjp(back_keep, back_low)
EPSILON = 1e-06
HIGHEST = lax.Precision.HIGHEST

def rms_apply(values, gain):
    return values * lax.rsqrt(lax.optimization_barrier(jnp.mean(values * values, axis=-1, keepdims=True)) + EPSILON) * gain

def layer_block(block_tokens, block_routes, norm_attn, qkv_weight, out_weight, norm_moe, router_weight, gate_up, down):
    seq_len = block_tokens.shape[0]
    model_width = block_tokens.shape[1]
    query_width = HEADS * HEAD_DIM
    kv_width = KV_HEADS * HEAD_DIM
    group_size = HEADS // KV_HEADS
    score_scale = HEAD_DIM ** (-0.5)
    xn_first = low(rms_apply(block_tokens, norm_attn))
    joint = low_back(low(jnp.dot(xn_first, qkv_weight, precision=HIGHEST)))
    queries = joint[:, :query_width].reshape(seq_len, KV_HEADS, group_size, HEAD_DIM)
    keys = joint[:, query_width:query_width + kv_width].reshape(seq_len, KV_HEADS, HEAD_DIM)
    values = joint[:, query_width + kv_width:].reshape(seq_len, KV_HEADS, HEAD_DIM)
    scores = low_back(jnp.einsum('qhgd,khd->hgqk', queries, keys, precision=HIGHEST) * score_scale)
    causal = jnp.arange(seq_len)[:, None] >= jnp.arange(seq_len)[None, :]
    scores = jnp.where(causal, scores, -1e+30)
    attn_probs = low(jax.nn.softmax(scores, axis=-1))
    attended = jnp.einsum('hgqk,khd->qhgd', attn_probs, values, precision=HIGHEST).reshape(seq_len, query_width)
    attended = low_back(low(attended))
    hidden = block_tokens + low_back(jnp.dot(attended, out_weight, precision=HIGHEST))
    xn_second = low(rms_apply(hidden, norm_moe))
    logits = low_back(jnp.dot(xn_second, router_weight, precision=HIGHEST))
    chosen_mask = block_routes[:, :, None] == jnp.arange(EXPERTS, dtype=jnp.int32)[None, None, :]
    chosen = lax.optimization_barrier(jnp.sum(jnp.where(chosen_mask, logits[:, None, :], 0.0), axis=-1))
    gate_probs = jax.nn.softmax(chosen, axis=-1)
    flat_mask = chosen_mask.reshape(seq_len * TOP, EXPERTS).astype(jnp.int32)
    before = jnp.cumsum(flat_mask, axis=0) - flat_mask
    slot_index = lax.optimization_barrier(jnp.sum(before * flat_mask, axis=-1))
    buffer_rows = (block_routes.reshape(-1) * CAP + slot_index).astype(jnp.int32)
    token_rows = (jnp.arange(seq_len * TOP, dtype=jnp.int32) // TOP).astype(jnp.int32)
    buffer = jnp.zeros((EXPERTS * CAP, model_width), xn_second.dtype).at[buffer_rows].set(xn_second[token_rows])
    buffer = low_back(buffer.reshape(EXPERTS, CAP, model_width))
    projected = low_back(jnp.einsum('ecd,edf->ecf', buffer, gate_up, precision=HIGHEST))
    inner_act = low(jax.nn.gelu(projected[..., :FFE]) * projected[..., FFE:])
    outputs = low_back(low(jnp.einsum('ecf,efd->ecd', inner_act, down, precision=HIGHEST)))
    returned = outputs.reshape(EXPERTS * CAP, model_width)[buffer_rows].reshape(seq_len, TOP, model_width)
    return hidden + lax.optimization_barrier(jnp.sum(gate_probs[:, :, None] * returned, axis=1))

def reference(tokens, routes, norm_attn, qkv_weight, out_weight, norm_moe, router_weight, gate_up, down, grad_output):
    block_count = TOKENS // TOK_DEV
    token_blocks = tokens.astype(jnp.float32).reshape(block_count, TOK_DEV, D)
    route_blocks = routes.reshape(block_count, TOK_DEV, TOP)

    def forward(token_arg, norm_a, qkv_w, out_w, norm_m, router_w, gate_up_w, down_w):

        def block_step(block_pair):
            return layer_block(block_pair[0], block_pair[1], norm_a, qkv_w, out_w, norm_m, router_w, gate_up_w, down_w)
        return lax.map(jax.checkpoint(block_step), (token_arg, route_blocks))
    layer_out, pullback = jax.vjp(forward, token_blocks, norm_attn.astype(jnp.float32), qkv_weight.astype(jnp.float32), out_weight.astype(jnp.float32), norm_moe.astype(jnp.float32), router_weight.astype(jnp.float32), gate_up.astype(jnp.float32), down.astype(jnp.float32))
    gradients = pullback(grad_output.astype(jnp.float32).reshape(block_count, TOK_DEV, D))
    return (layer_out.reshape(TOKENS, D).astype(jnp.bfloat16), gradients[0].reshape(TOKENS, D), gradients[1], gradients[2], gradients[3], gradients[4], gradients[5], gradients[6], gradients[7])
```

```python
import jax
import jax.numpy as jnp
from jax import lax
from jax.sharding import PartitionSpec as P

HEADS = 12
KV_HEADS = 2
HEAD_DIM = 128
FFE = 768
EXPERTS = 32
TOP = 4
CAP = 48
EPSILON = 1e-06
BOTH = ("expert", "fsdp")
f32 = jnp.float32
bf16 = jnp.bfloat16


def dot(a, b):
    return jnp.dot(a, b, preferred_element_type=f32)


def dot_t(a, b):
    return lax.dot_general(a, b, (((1,), (1,)), ((), ())), preferred_element_type=f32)


def t_dot(a, b):
    return lax.dot_general(a, b, (((0,), (0,)), ((), ())), preferred_element_type=f32)


def rms_apply(values, gain):
    return values * lax.rsqrt(jnp.mean(values * values, axis=-1, keepdims=True) + EPSILON) * gain


def reglu_smooth(projected):
    return jax.nn.gelu(projected[..., :FFE]) * projected[..., FFE:]


def attention_probs(queries, keys):
    seq_len = queries.shape[0]
    scores = jnp.einsum("qhgd,khd->hgqk", queries, keys, preferred_element_type=f32) * HEAD_DIM ** (-0.5)
    causal = jnp.arange(seq_len)[:, None] >= jnp.arange(seq_len)[None, :]
    scores = jnp.where(causal, scores, -1e30)
    row_max = jnp.max(scores, axis=-1, keepdims=True)
    exponent = jnp.exp(scores - row_max)
    return exponent / jnp.sum(exponent, axis=-1, keepdims=True)


def attend_backward(queries, keys, values, grad_heads):
    seq_len = queries.shape[0]
    score_scale = HEAD_DIM ** (-0.5)
    attn_full = attention_probs(queries, keys)
    attn_probs = attn_full.astype(bf16)
    grad_probs = jnp.einsum("qhgd,khd->hgqk", grad_heads, values, preferred_element_type=f32)
    delta = jnp.sum(attn_full * grad_probs, axis=-1, keepdims=True)
    grad_scores = (attn_full * (grad_probs - delta)).astype(bf16)
    grad_query = jnp.einsum("hgqk,khd->qhgd", grad_scores, keys, preferred_element_type=f32) * score_scale
    grad_keys = jnp.einsum("hgqk,qhgd->khd", grad_scores, queries, preferred_element_type=f32) * score_scale
    grad_values = jnp.einsum("hgqk,qhgd->khd", attn_probs, grad_heads, preferred_element_type=f32)
    return (
        grad_query.reshape(seq_len, -1),
        grad_keys.reshape(seq_len, -1),
        grad_values.reshape(seq_len, -1),
    )


def shards(
    tokens,
    routes,
    norm_attn,
    qkv_weight,
    out_weight,
    norm_moe,
    router_weight,
    gate_up,
    down,
    grad_output,
):
    seq_len, model_width = tokens.shape
    query_width = HEADS * HEAD_DIM
    kv_width = KV_HEADS * HEAD_DIM
    group_size = HEADS // KV_HEADS
    fsdp = lax.axis_size("fsdp")
    devices = lax.axis_size("expert") * fsdp
    local_count = gate_up.shape[0]
    parts = fsdp // local_count
    rows = EXPERTS * CAP

    def to_owner(weight):
        whole = weight
        if parts > 1:
            whole = jnp.repeat(weight, parts, axis=0)
        return lax.all_to_all(whole, "fsdp", split_axis=0, concat_axis=0, tiled=True).reshape(
            -1, weight.shape[-1]
        )

    def to_shards(grad, like):
        back = lax.all_to_all(
            grad.reshape(fsdp, like.shape[1], like.shape[2]), "fsdp", split_axis=0, concat_axis=0, tiled=True
        ).astype(f32)
        if parts > 1:
            back = jnp.sum(back.reshape((local_count, parts) + like.shape[1:]), axis=1)
        return back

    def exchange(buffer):
        width = buffer.shape[-1]
        return lax.all_to_all(
            buffer.reshape(devices, rows // devices, width), BOTH, split_axis=0, concat_axis=0, tiled=True
        ).reshape(rows, width)

    token_f = tokens.astype(f32)
    grad_f = grad_output.astype(f32)
    qkv_full, out_full = (
        lax.all_gather(qkv_weight, "fsdp", axis=0, tiled=True),
        lax.all_gather(out_weight, "fsdp", axis=0, tiled=True),
    )

    expert_ids = jnp.arange(EXPERTS, dtype=jnp.int32)
    chosen_mask = routes[:, :, None] == expert_ids[None, None, :]
    mask = jnp.any(chosen_mask, axis=1)
    mask_b = mask.astype(bf16)
    order = jnp.arange(seq_len)
    earlier = (order[None, :] < order[:, None]).astype(bf16)
    position = dot(earlier, mask_b).astype(jnp.int32)
    slot = jnp.where(mask, position, -1).T
    place = (slot[:, None, :] == jnp.arange(CAP, dtype=jnp.int32)[None, :, None]).astype(bf16)
    place = place.reshape(rows, seq_len)

    grad_rows = exchange(dot(place, grad_output).astype(bf16))
    gate_up_full = to_owner(gate_up)
    down_full = to_owner(down)

    xn_first_f, norm_first_pull = jax.vjp(rms_apply, token_f, norm_attn)
    xn_first = xn_first_f.astype(bf16)
    joint = dot(xn_first, qkv_full).astype(bf16)
    queries = joint[:, :query_width].reshape(seq_len, KV_HEADS, group_size, HEAD_DIM)
    keys = joint[:, query_width : query_width + kv_width].reshape(seq_len, KV_HEADS, HEAD_DIM)
    values = joint[:, query_width + kv_width :].reshape(seq_len, KV_HEADS, HEAD_DIM)
    probs = attention_probs(queries, keys).astype(bf16)
    attended = (
        jnp.einsum("hgqk,khd->qhgd", probs, values, preferred_element_type=f32)
        .astype(bf16)
        .reshape(seq_len, query_width)
    )
    hidden = token_f + dot(attended, out_full)
    xn_second_f, norm_second_pull = jax.vjp(rms_apply, hidden, norm_moe)
    xn_second = xn_second_f.astype(bf16)

    logits = dot(xn_second, router_weight)
    masked = jnp.where(mask, logits, -1e30)
    exponent = jnp.where(mask, jnp.exp(masked - jnp.max(masked, axis=-1, keepdims=True)), 0.0)
    gates = exponent / jnp.sum(exponent, axis=-1, keepdims=True)

    received = exchange(dot(place, xn_second).astype(bf16))
    place_cube = place.reshape(EXPERTS, CAP, seq_len).astype(f32)
    gate_send = jnp.sum(place_cube * gates.T[:, None, :], axis=-1)
    gate_rows = exchange(gate_send.reshape(rows, 1))

    projected = dot(received, gate_up_full)
    inner, reglu_pull = jax.vjp(reglu_smooth, projected)
    inner = inner.astype(bf16)
    expert_out = dot(inner, down_full).astype(bf16)
    d_gate_rows = jnp.sum(expert_out.astype(f32) * grad_rows.astype(f32), axis=-1, keepdims=True)
    d_out = (gate_rows * grad_rows.astype(f32)).astype(bf16)
    d_inner = dot_t(d_out, down_full)
    d_projected = reglu_pull(d_inner)[0].astype(bf16)
    d_pair_in = dot_t(d_projected, gate_up_full).astype(bf16)
    grad_down = to_shards(t_dot(inner, d_out).astype(bf16), down)
    grad_gate_up = to_shards(t_dot(received, d_projected).astype(bf16), gate_up)

    back_in = exchange(d_pair_in)
    back_gate = exchange(d_gate_rows)
    back_out = exchange(expert_out)

    gate_place = jnp.where(place_cube > 0, gates.T[:, None, :], 0.0).reshape(rows, seq_len)
    gate_hi = gate_place.astype(bf16)
    gate_lo = (gate_place - gate_hi.astype(f32)).astype(bf16)
    moe_sum = t_dot(gate_hi, back_out) + t_dot(gate_lo, back_out)
    mixed = (hidden + moe_sum).astype(bf16)
    d_gates = jnp.sum(place_cube * back_gate.reshape(EXPERTS, CAP, 1), axis=1).T
    d_chosen = gates * (d_gates - jnp.sum(gates * d_gates, axis=-1, keepdims=True))
    d_logits = d_chosen.astype(bf16)
    router_local = t_dot(xn_second, d_logits)
    d_xn_second = dot_t(d_logits, router_weight) + t_dot(place, back_in)

    d_hidden_norm, gain_moe_local = norm_second_pull(d_xn_second)
    d_hidden = grad_f + d_hidden_norm
    d_hidden_b = d_hidden.astype(bf16)
    out_local = t_dot(attended, d_hidden_b)
    d_attended = dot_t(d_hidden_b, out_full).astype(bf16)
    grad_heads = d_attended.reshape(seq_len, KV_HEADS, group_size, HEAD_DIM)
    grad_query, grad_keys, grad_values = attend_backward(queries, keys, values, grad_heads)
    grad_joint = jnp.concatenate([grad_query, grad_keys, grad_values], axis=1).astype(bf16)
    qkv_local = t_dot(xn_first, grad_joint)
    d_xn_first = dot_t(grad_joint, qkv_full)
    d_token_norm, gain_attn_local = norm_first_pull(d_xn_first)
    grad_tokens = d_hidden + d_token_norm

    sectioned = (
        lax.psum_scatter(qkv_local.astype(bf16), "fsdp", scatter_dimension=0, tiled=True),
        lax.psum_scatter(out_local.astype(bf16), "fsdp", scatter_dimension=0, tiled=True),
    )
    grad_qkv, grad_out_proj = (
        lax.psum(sectioned[0], "expert").astype(f32),
        lax.psum(sectioned[1], "expert").astype(f32),
    )
    grad_norm_attn, grad_norm_moe, grad_router = lax.psum(
        (gain_attn_local, gain_moe_local, router_local), BOTH
    )
    return (
        mixed,
        grad_tokens,
        grad_norm_attn,
        grad_qkv,
        grad_out_proj,
        grad_norm_moe,
        grad_router,
        grad_gate_up,
        grad_down,
    )


def solution(mesh):
    in_specs = (
        P(BOTH, None),
        P(BOTH, None),
        P(),
        P("fsdp", None),
        P("fsdp", None),
        P(),
        P(),
        P("expert", "fsdp", None),
        P("expert", "fsdp", None),
        P(BOTH, None),
    )
    out_specs = (
        P(BOTH, None),
        P(BOTH, None),
        P(),
        P("fsdp", None),
        P("fsdp", None),
        P(),
        P(),
        P("expert", "fsdp", None),
        P("expert", "fsdp", None),
    )
    return jax.shard_map(shards, mesh=mesh, in_specs=in_specs, out_specs=out_specs, check_vma=False)
```

```python
import jax
import jax.numpy as jnp
from jax import lax
from jax.experimental import pallas as pl
from jax.experimental.pallas import tpu as pltpu
from jax.sharding import Mesh
from jax.sharding import PartitionSpec as P

HEADS = 12
KV_HEADS = 2
HEAD_DIM = 128
FFE = 768
EXPERTS = 32
TOP = 4
CAP = 48
EPSILON = 1e-06
VMEM_LIMIT = 56 * 1024 * 1024
EXTRA = 128
EXPERT = ("y", "c")
FSDP = ("h", "r")
BOTH = EXPERT + FSDP
HALF = ("y", "c", "r")
f32 = jnp.float32
bf16 = jnp.bfloat16


def dot(a, b):
    return jnp.dot(a, b, preferred_element_type=f32)


def dot_t(a, b):
    return lax.dot_general(a, b, (((1,), (1,)), ((), ())), preferred_element_type=f32)


def t_dot(a, b):
    return lax.dot_general(a, b, (((0,), (0,)), ((), ())), preferred_element_type=f32)


def rms_apply(values, gain):
    return values * lax.rsqrt(jnp.mean(values * values, axis=-1, keepdims=True) + EPSILON) * gain


def reglu_smooth(projected):
    return jax.nn.gelu(projected[..., :FFE]) * projected[..., FFE:]


def swap(value, axis, bit=1):
    size = lax.axis_size(axis)
    return lax.ppermute(value, axis, [(i, i ^ bit) for i in range(size)])


def sum_over(value, axes):
    for axis in axes:
        bit = 1
        while bit < lax.axis_size(axis):
            value = value + swap(value, axis, bit)
            bit *= 2
    return value


def together(*values):
    return lax.optimization_barrier(values)


def marker_kernel(*refs):
    pass


def mark(values):
    flat, tree = jax.tree.flatten(values)
    anywhere = [pl.BlockSpec(memory_space=pl.ANY)] * len(flat)
    same = pl.pallas_call(
        marker_kernel,
        in_specs=anywhere,
        out_specs=anywhere,
        out_shape=[jax.ShapeDtypeStruct(value.shape, value.dtype) for value in flat],
        input_output_aliases={number: number for number in range(len(flat))},
        cost_estimate=pl.CostEstimate(flops=10**12, bytes_accessed=0, transcendentals=0),
    )(*flat)
    return jax.tree.unflatten(tree, same)


def order_by(index, mine, other, axis):
    size = mine.shape[axis]
    shape = mine.shape[:axis] + (2 * size,) + mine.shape[axis + 1 :]
    start = [0] * mine.ndim
    start[axis] = index * size
    both = lax.dynamic_update_slice(jnp.zeros(shape, mine.dtype), mine, start)
    start[axis] = (1 - index) * size
    return lax.dynamic_update_slice(both, other, start)


def part_of(value, index, axis):
    size = value.shape[axis] // 2
    return lax.dynamic_slice_in_dim(value, index * size, size, axis=axis)


def split_width(width):
    first = (width // 2 + 127) // 128 * 128
    return first, width - first


def fsdp_bits():
    size = lax.axis_size("r")
    bits = [("h", 1, 0)]
    bit = size // 2
    while bit:
        bits.append(("r", bit, len(bits)))
        bit //= 2
    return bits


def bit_index(axis, bit):
    return (lax.axis_index(axis) // bit) % 2


def gather_step(block, step):
    axis, bit, dim = step
    return order_by(bit_index(axis, bit), block, swap(block, axis, bit), dim)


def scatter_step(block, step):
    axis, bit, dim = step
    index = bit_index(axis, bit)
    other = swap(part_of(block, 1 - index, dim).astype(bf16), axis, bit)
    return part_of(block, index, dim).astype(f32) + other.astype(f32)


def gather_shards(shard, first_done):
    steps = fsdp_bits()
    rows, columns = shard.shape
    whole_rows = rows * lax.axis_size(FSDP)
    shape = (1,) * len(steps) + (rows, columns)
    if lax.axis_size("y") != 2:
        block = shard.reshape(shape)
        for step in steps:
            block = gather_step(block, step)
        return first_done(block).reshape(whole_rows, columns)
    lane = len(steps) + 1
    y_step, x_step = ("y", 1, lane), steps[-1]
    block = part_of(shard.reshape(shape), lax.axis_index("y"), lane)
    for step in steps[:-1]:
        block = gather_step(block, step)
    block = first_done(block)
    first, last = jnp.split(block, [split_width(columns // 2)[0]], axis=lane)
    first, last = gather_step(first, x_step), gather_step(last, y_step)
    first, last = gather_step(first, y_step), gather_step(last, x_step)
    parts = [
        piece for pair in zip(jnp.split(first, 2, axis=lane), jnp.split(last, 2, axis=lane)) for piece in pair
    ]
    return jnp.concatenate(parts, axis=lane).reshape(whole_rows, columns)


def scatter_sends(left, right):
    if lax.axis_size("y") != 2:
        return None
    x_step = fsdp_bits()[-1]
    left_of, right_of, right_last = product_parts(left, right)
    y_index, x_index = lax.axis_index("y"), bit_index(*x_step[:2])
    return (
        swap(t_dot(left, right_of(1 - y_index)).astype(bf16), "y"),
        swap(t_dot(left_of(1 - x_index), right_last).astype(bf16), *x_step[:2]),
    )


def product_parts(left, right):
    tokens, whole_rows = left.shape
    columns = right.shape[1]
    rows = whole_rows // lax.axis_size(FSDP)
    width = split_width(columns // 2)[0]
    left_blocks = left.reshape(tokens, -1, 2, rows)
    cube = right.reshape(tokens, 2, columns // 2)
    right_first, right_last = cube[:, :, :width], cube[:, :, width:].reshape(tokens, -1)

    def left_of(index):
        return lax.dynamic_index_in_dim(left_blocks, index, 2, keepdims=False).reshape(tokens, -1)

    def right_of(index):
        return lax.dynamic_index_in_dim(right_first, index, 1, keepdims=False)

    return left_of, right_of, right_last


def scatter_products(pairs, sends, rounds):
    steps = fsdp_bits()
    size = lax.axis_size(FSDP)
    if lax.axis_size("y") != 2:
        blocks = [t_dot(left, right) for left, right in pairs]
        blocks = [block.reshape((2,) * len(steps) + (block.shape[0] // size, -1)) for block in blocks]
        for number, step in enumerate(reversed(steps)):
            blocks = [scatter_step(block, step) for block in blocks]
            if number < 2:
                blocks = rounds[number](blocks)
        blocks = rounds[2](blocks)
        blocks = [block.astype(bf16).reshape(block.shape[-2:]) for block in blocks]
        return [sum_over(block, ("y",)).astype(bf16) for block in blocks]
    lane = len(steps) + 1
    y_step, x_step = ("y", 1, lane), steps[-1]
    y_index, x_index = lax.axis_index("y"), bit_index(*x_step[:2])
    firsts, lasts = [], []
    for (left, right), (first_sent, last_sent) in zip(pairs, sends):
        left_of, right_of, right_last = product_parts(left, right)
        rows = left.shape[1] // size
        first = t_dot(left, right_of(y_index)) + first_sent.astype(f32)
        last = t_dot(left_of(x_index), right_last) + last_sent.astype(f32)
        firsts.append(first.reshape((2,) * len(steps) + (rows, -1)))
        lasts.append(last.reshape((2,) * (len(steps) - 1) + (1, rows, 2, last.shape[1] // 2)))
    widths = [block.shape[-1] for block in firsts + lasts]
    first = jnp.concatenate(firsts, axis=lane)
    last = jnp.concatenate(lasts, axis=lane + 1)
    last = last.reshape(last.shape[:lane] + (-1,))
    first, last = rounds[0]((first, last))
    first, last = scatter_step(first, x_step), scatter_step(last, y_step)
    block = rounds[1](jnp.concatenate([first, last], axis=lane))
    for step in reversed(steps[:-1]):
        block = scatter_step(block, step)
    block = rounds[2](block).astype(bf16).reshape(block.shape[-2:])
    cuts = [sum(widths[: number + 1]) for number in range(len(widths) - 1)]
    halves = [jnp.split(half, cuts, axis=1) for half in jnp.split(order_by(y_index, block, swap(block, "y"), 1), 2, axis=1)]
    count = len(pairs)
    return [
        jnp.concatenate([half[number + part] for half in halves for part in (0, count)], axis=1)
        for number in range(count)
    ]


def head_probs(query, key):
    seq_len = query.shape[0]
    scores = dot_t(query, key) * HEAD_DIM ** (-0.5)
    rows = lax.broadcasted_iota(jnp.int32, (seq_len, seq_len), 0)
    columns = lax.broadcasted_iota(jnp.int32, (seq_len, seq_len), 1)
    scores = jnp.where(rows >= columns, scores, -1e30)
    exponent = jnp.exp(scores - jnp.max(scores, axis=-1, keepdims=True))
    return exponent / jnp.sum(exponent, axis=-1, keepdims=True)


def attend_kernel(xn_ref, weight_ref, joint_ref, attended_ref):
    joint = dot(xn_ref[...], weight_ref[...]).astype(bf16)
    joint_ref[...] = joint
    width = HEADS // 2 * HEAD_DIM
    key, value = joint[:, width : width + HEAD_DIM], joint[:, width + HEAD_DIM :]
    for head in range(HEADS // 2):
        columns = slice(head * HEAD_DIM, (head + 1) * HEAD_DIM)
        probs = head_probs(joint[:, columns], key).astype(bf16)
        attended_ref[:, columns] = dot(probs, value).astype(bf16)


def attend(xn_pair, weight, seq_len):
    rows, model_width = xn_pair.shape
    width = weight.shape[1]
    query_width = HEADS // 2 * HEAD_DIM
    return pl.pallas_call(
        attend_kernel,
        grid=(rows // seq_len,),
        in_specs=[
            pl.BlockSpec((seq_len, model_width), lambda i: (i, 0)),
            pl.BlockSpec((model_width, width), lambda i: (0, 0)),
        ],
        out_specs=[
            pl.BlockSpec((seq_len, width), lambda i: (i, 0)),
            pl.BlockSpec((seq_len, query_width), lambda i: (i, 0)),
        ],
        out_shape=[
            jax.ShapeDtypeStruct((rows, width), bf16),
            jax.ShapeDtypeStruct((rows, query_width), bf16),
        ],
        compiler_params=pltpu.CompilerParams(vmem_limit_bytes=VMEM_LIMIT),
        cost_estimate=pl.CostEstimate(flops=0, bytes_accessed=0, transcendentals=0),
    )(xn_pair, weight)


def attend_backward_kernel(joint_ref, grad_ref, weight_ref, grad_joint_ref, grad_xn_ref):
    scale = HEAD_DIM ** (-0.5)
    width = HEADS // 2 * HEAD_DIM
    joint = joint_ref[...]
    grad = grad_ref[...]
    key, value = joint[:, width : width + HEAD_DIM], joint[:, width + HEAD_DIM :]
    grad_key = jnp.zeros(key.shape, f32)
    grad_value = jnp.zeros(value.shape, f32)
    for head in range(HEADS // 2):
        columns = slice(head * HEAD_DIM, (head + 1) * HEAD_DIM)
        query, grad_head = joint[:, columns], grad[:, columns]
        probs = head_probs(query, key)
        grad_probs = dot_t(grad_head, value)
        delta = jnp.sum(probs * grad_probs, axis=-1, keepdims=True)
        grad_scores = (probs * (grad_probs - delta)).astype(bf16)
        grad_joint_ref[:, columns] = (dot(grad_scores, key) * scale).astype(bf16)
        grad_key = grad_key + t_dot(grad_scores, query)
        grad_value = grad_value + t_dot(probs.astype(bf16), grad_head)
    grad_joint_ref[:, width : width + HEAD_DIM] = (grad_key * scale).astype(bf16)
    grad_joint_ref[:, width + HEAD_DIM :] = grad_value.astype(bf16)
    grad_xn_ref[...] = dot_t(grad_joint_ref[...], weight_ref[...])


def attend_backward(joint, grad_attended, weight, seq_len):
    rows, width = joint.shape
    model_width = weight.shape[0]
    query_width = HEADS // 2 * HEAD_DIM
    return pl.pallas_call(
        attend_backward_kernel,
        grid=(rows // seq_len,),
        in_specs=[
            pl.BlockSpec((seq_len, width), lambda i: (i, 0)),
            pl.BlockSpec((seq_len, query_width), lambda i: (i, 0)),
            pl.BlockSpec((model_width, width), lambda i: (0, 0)),
        ],
        out_specs=[
            pl.BlockSpec((seq_len, width), lambda i: (i, 0)),
            pl.BlockSpec((seq_len, model_width), lambda i: (i, 0)),
        ],
        out_shape=[
            jax.ShapeDtypeStruct((rows, width), bf16),
            jax.ShapeDtypeStruct((rows, model_width), f32),
        ],
        compiler_params=pltpu.CompilerParams(vmem_limit_bytes=VMEM_LIMIT),
        cost_estimate=pl.CostEstimate(flops=0, bytes_accessed=0, transcendentals=0),
    )(joint, grad_attended, weight)


def expert_kernel(
    expert_ref,
    rows_ref,
    grad_ref,
    router_ref,
    up_ref,
    down_ref,
    inner_ref,
    out_ref,
    d_out_ref,
    d_projected_ref,
    d_in_ref,
):
    rows = rows_ref[...]
    width = rows.shape[1]
    mask = grad_ref[:, width : width + EXPERTS] > 0
    logits = jnp.where(mask, dot(rows, router_ref[...]), -1e30)
    exponent = jnp.where(mask, jnp.exp(logits - jnp.max(logits, axis=-1, keepdims=True)), 0.0)
    total = jnp.sum(exponent, axis=-1, keepdims=True)
    mine = lax.broadcasted_iota(jnp.int32, exponent.shape, 1) == expert_ref[0]
    gate = jnp.sum(jnp.where(mine, exponent, 0.0), axis=-1, keepdims=True)
    gate = gate / jnp.where(total > 0, total, 1.0)

    projected = dot(rows, up_ref[...])
    lower, upper = projected[:, :FFE], projected[:, FFE:]
    slope = (2.0 / 3.141592653589793) ** 0.5
    bend = jnp.tanh(slope * (lower + 0.044715 * lower * lower * lower))
    gelu = 0.5 * lower * (1.0 + bend)
    gelu_grad = 0.5 * (1.0 + bend) + 0.5 * lower * (1.0 - bend * bend) * slope * (
        1.0 + 3 * 0.044715 * lower * lower
    )
    inner = (gelu * upper).astype(bf16)
    inner_ref[...] = inner
    out = dot(inner, down_ref[...]).astype(bf16)
    out_ref[...] = out
    grad = grad_ref[:, :width].astype(f32)
    d_gate = jnp.sum(out.astype(f32) * grad, axis=-1, keepdims=True)
    d_gate_high = d_gate.astype(bf16).astype(f32)
    column = lax.broadcasted_iota(jnp.int32, (rows.shape[0], EXTRA), 1)
    d_in_ref[:, width:] = jnp.where(
        column == expert_ref[1],
        d_gate_high,
        jnp.where(column == expert_ref[1] + EXPERTS // 2, d_gate - d_gate_high, 0.0),
    ).astype(bf16)
    d_out = (gate * grad).astype(bf16)
    d_out_ref[...] = d_out
    d_inner = dot_t(d_out, down_ref[...])
    d_projected_ref[:, :FFE] = (d_inner * upper * gelu_grad).astype(bf16)
    d_projected_ref[:, FFE:] = (d_inner * gelu).astype(bf16)
    d_in_ref[:, :width] = dot_t(d_projected_ref[...], up_ref[...]).astype(bf16)


def expert_part(expert, received, grad_rows, router, up, down):
    rows, model_width = received.shape
    block = 256

    def row_block(width):
        return pl.BlockSpec((block, width), lambda i, *_: (i, 0))

    def whole(array):
        return pl.BlockSpec(array.shape, lambda i, *_: (0, 0))

    widths = (FFE, model_width, model_width, 2 * FFE, model_width + EXTRA)
    return pl.pallas_call(
        expert_kernel,
        grid_spec=pltpu.PrefetchScalarGridSpec(
            num_scalar_prefetch=1,
            grid=(rows // block,),
            in_specs=[
                row_block(model_width),
                row_block(model_width + EXTRA),
                whole(router),
                whole(up),
                whole(down),
            ],
            out_specs=[row_block(width) for width in widths],
        ),
        out_shape=[jax.ShapeDtypeStruct((rows, width), bf16) for width in widths],
        compiler_params=pltpu.CompilerParams(vmem_limit_bytes=VMEM_LIMIT),
        cost_estimate=pl.CostEstimate(flops=0, bytes_accessed=0, transcendentals=0),
    )(expert, received, grad_rows, router, up, down)


def expert_weights_kernel(x_own, x_far, p_own, p_far, i_own, i_far, d_own, d_far, up_ref, down_ref):
    up_ref[...] = (t_dot(x_own[...], p_own[...]) + t_dot(x_far[...], p_far[...])).astype(bf16)
    down_ref[...] = (t_dot(i_own[...], d_own[...]) + t_dot(i_far[...], d_far[...])).astype(bf16)


def expert_weights(received, d_projected, inner, d_out):
    rows, model_width = received[0].shape
    steps = 3

    def columns(array):
        return pl.BlockSpec((rows, array.shape[1] // steps), lambda i: (0, i))

    def whole(array):
        return pl.BlockSpec(array.shape, lambda i: (0, 0))

    return pl.pallas_call(
        expert_weights_kernel,
        grid=(steps,),
        in_specs=[columns(a) for a in received]
        + [whole(a) for a in d_projected]
        + [columns(a) for a in inner]
        + [whole(a) for a in d_out],
        out_specs=[
            pl.BlockSpec((model_width // steps, 2 * FFE), lambda i: (i, 0)),
            pl.BlockSpec((FFE // steps, model_width), lambda i: (i, 0)),
        ],
        out_shape=[
            jax.ShapeDtypeStruct((model_width, 2 * FFE), bf16),
            jax.ShapeDtypeStruct((FFE, model_width), bf16),
        ],
        compiler_params=pltpu.CompilerParams(vmem_limit_bytes=VMEM_LIMIT),
        cost_estimate=pl.CostEstimate(flops=0, bytes_accessed=0, transcendentals=0),
    )(*received, *d_projected, *inner, *d_out)


def shards(
    tokens,
    routes,
    norm_attn,
    qkv_weight,
    out_weight,
    norm_moe,
    router_weight,
    gate_up,
    down,
    grad_output,
):
    seq_len, model_width = tokens.shape
    query_half = HEADS * HEAD_DIM // 2
    kv_half = KV_HEADS * HEAD_DIM // 2
    out_half = out_weight.shape[1] // 2
    groups = lax.axis_size(EXPERT)
    fsdp = lax.axis_size(FSDP)
    half_devices = groups * fsdp // 2
    local_count = gate_up.shape[0]
    parts = fsdp // local_count
    half_experts = EXPERTS // 2
    rows = half_experts * CAP
    core = lax.axis_index("c")
    half = lax.axis_index("h")
    me = lax.axis_index(FSDP)
    group = lax.axis_index(EXPERT)
    my_expert = jnp.stack(
        [
            group * local_count + me // parts,
            group * (local_count // 2) + me // parts - half * (local_count // 2),
        ]
    ).astype(jnp.int32)

    def fsdp_partner(value, bit):
        return lax.ppermute(value, FSDP, [(i, i ^ bit) for i in range(fsdp)])

    box = {}

    def tie(value, *names):
        value, held = together(value, [box[name] for name in names])
        box.update(zip(names, held))
        return value

    up_width, down_width = gate_up.shape[1], down.shape[1]
    even, odd = [list(range(fsdp // 2 + first, fsdp, 2)) for first in range(2)]
    middle = len(even) // 2
    turns = [even[:middle], even[middle:], odd[:middle], odd[middle:]]
    near = [list(range(1, fsdp // 2))[turn::3] for turn in range(3)]

    def fetch(bits, *names):
        for bit in bits:
            expert = (me ^ bit) // parts
            piece = jnp.concatenate(
                [
                    lax.dynamic_index_in_dim(gate_up, expert, 0, keepdims=False),
                    lax.dynamic_index_in_dim(down, expert, 0, keepdims=False),
                ],
                axis=0,
            )
            box["in", bit] = fsdp_partner(tie(piece, *names), bit) if bit else piece

    def coming(bits):
        return [("in", bit) for bit in bits]

    def assemble():
        up_full = jnp.zeros((fsdp * up_width, gate_up.shape[2]), gate_up.dtype)
        down_full = jnp.zeros((fsdp * down_width, down.shape[2]), down.dtype)
        for bit in [0] + near[1] + turns[0] + near[0] + turns[1] + turns[2] + turns[3] + near[2]:
            other, piece = me ^ bit, box["in", bit]
            up_full = lax.dynamic_update_slice(up_full, piece[:up_width], (other * up_width, 0))
            down_full = lax.dynamic_update_slice(down_full, piece[up_width:], (other * down_width, 0))
        return up_full, down_full

    columns = fsdp // 4
    stay = [(0, 0)]
    same = [(1, 0), (3, 0), (2, 0)]
    across = [(step, cross) for cross in range(1, columns) for step in (1, 3)]
    opposite = [(2, cross) for cross in range(1, columns)]
    level = [(0, cross) for cross in range(1, columns)]

    def target(index, move, sign=1):
        step, cross = move
        return (index // columns + sign * step + 4) % 4 * columns + (index % columns ^ cross)

    def give(moves, up_grad, down_grad, *names):
        for move in moves:
            to = target(me, move)
            piece = jnp.concatenate(
                [
                    lax.dynamic_slice_in_dim(up_grad, to * up_width, up_width, axis=0),
                    lax.dynamic_slice_in_dim(down_grad, to * down_width, down_width, axis=0),
                ],
                axis=0,
            )
            if move != (0, 0):
                piece = lax.ppermute(tie(piece, *names), FSDP, [(i, target(i, move)) for i in range(fsdp)])
            box["out", move] = piece

    def going(moves):
        return [("out", move) for move in moves]

    def collect():
        up_sum = jnp.zeros(gate_up.shape, f32)
        down_sum = jnp.zeros(down.shape, f32)
        for move in stay + same + opposite + across + level:
            expert = target(me, move, -1) // parts
            piece = box["out", move].astype(f32)[None]
            up_part, down_part = piece[:, :up_width], piece[:, up_width:]
            if parts > 1:
                up_part = up_part + lax.dynamic_slice_in_dim(up_sum, expert, 1, axis=0)
                down_part = down_part + lax.dynamic_slice_in_dim(down_sum, expert, 1, axis=0)
            up_sum = lax.dynamic_update_slice(up_sum, up_part, (expert, 0, 0))
            down_sum = lax.dynamic_update_slice(down_sum, down_part, (expert, 0, 0))
        return up_sum, down_sum

    def exchange(buffer):
        shape = buffer.shape
        return lax.all_to_all(
            buffer.reshape((half_devices, rows // half_devices) + shape[1:]),
            HALF,
            split_axis=0,
            concat_axis=0,
            tiled=True,
        ).reshape(shape)

    def half_columns(table, index):
        cube = table.reshape(table.shape[0], groups, 2, local_count // 2)
        return lax.dynamic_index_in_dim(cube, index, 2, keepdims=False).reshape(table.shape[0], half_experts)

    def both_columns(mine, other):
        shape = (mine.shape[0], groups, 1, local_count // 2)
        return order_by(half, mine.reshape(shape), other.reshape(shape), 2).reshape(-1, EXPERTS)

    token_f = tokens.astype(f32)
    grad_f = grad_output.astype(f32)

    qkv_mine = jnp.concatenate(
        [
            lax.dynamic_slice_in_dim(qkv_weight, core * query_half, query_half, axis=1),
            lax.dynamic_slice_in_dim(qkv_weight, 2 * query_half + core * kv_half, kv_half, axis=1),
            lax.dynamic_slice_in_dim(qkv_weight, 2 * query_half + (2 + core) * kv_half, kv_half, axis=1),
        ],
        axis=1,
    )
    out_mine = lax.dynamic_slice_in_dim(out_weight, core * out_half, out_half, axis=1)
    expert_ids = jnp.arange(EXPERTS, dtype=jnp.int32)
    order = jnp.arange(seq_len)
    earlier = (order[None, :] < order[:, None]).astype(bf16)

    def placing(routing):
        mask = jnp.any(routing[:, :, None] == expert_ids[None, None, :], axis=1)
        position = dot(earlier, mask.astype(bf16)).astype(jnp.int32)
        slot = half_columns(jnp.where(mask, position, -1), half).T
        place = slot[:, None, :] == jnp.arange(CAP, dtype=jnp.int32)[None, :, None]
        return mask, place

    mask_own, cube_own = placing(routes)
    mask_far, cube_far = placing(swap(routes, "h"))
    place_own = cube_own.astype(bf16).reshape(rows, seq_len)
    place_far = cube_far.astype(bf16).reshape(rows, seq_len)

    def first_done(block):
        nonlocal gate_up, down
        sent, block, gate_up, down = together(grad_output, block, gate_up, down)
        box["grad_far"] = swap(sent, "h")
        fetch(near[1] + turns[0])
        return mark(block)

    def send_rows(place, grad, mask):
        extra = jnp.pad(mask.astype(bf16), ((0, 0), (0, EXTRA - EXPERTS)))
        return dot(place, jnp.concatenate([grad, extra], axis=1)).astype(bf16)

    xn_first_f, norm_first_pull = jax.vjp(rms_apply, token_f, norm_attn)
    xn_first = xn_first_f.astype(bf16)
    xn_pair = jnp.concatenate([xn_first, swap(xn_first, "c")], axis=0)
    shard = jnp.concatenate([qkv_mine, out_mine], axis=1)
    core_weights, xn_pair, own_sent = tie(
        (gather_shards(shard, first_done), xn_pair, send_rows(place_own, grad_output, mask_own)),
        "grad_far",
        *coming(turns[0] + near[1]),
    )
    box["grad_rows_own"] = exchange(own_sent)
    fetch(turns[1] + near[0], *coming(turns[0]))
    xn_pair = mark(xn_pair)
    qkv_width = query_half + 2 * kv_half
    qkv_core, out_core = core_weights[:, :qkv_width], core_weights[:, qkv_width:]

    joint, attended_mine = attend(xn_pair, qkv_core, seq_len)
    out_full = order_by(core, out_core, swap(out_core, "c"), 1)
    attended_mine = attended_mine.reshape(2, seq_len, query_half)
    far_sent = send_rows(place_far, box["grad_far"], mask_far)
    attended_mine, far_sent = tie((attended_mine, far_sent), "grad_rows_own", *coming(turns[1] + near[0]))
    box["grad_rows_far"] = exchange(far_sent)
    fetch(turns[2], *coming(turns[1]))
    attended_mine = mark(attended_mine)
    attended_other = swap(attended_mine, "c")
    attended = order_by(core, attended_mine[0], attended_other[1], 1)
    attended_next = order_by(core, attended_mine[1], attended_other[0], 1)
    hidden = token_f + dot(attended, out_full)
    xn_second_f, norm_second_pull = jax.vjp(rms_apply, hidden, norm_moe)
    xn_second = xn_second_f.astype(bf16)

    def gating(values_b, mask):
        logits = dot(values_b, router_weight)
        top = jnp.max(jnp.where(mask, logits, -1e30), axis=-1, keepdims=True)
        exponent = jnp.where(mask, jnp.exp(jnp.where(mask, logits - top, 0.0)), 0.0)
        total = jnp.sum(exponent, axis=-1, keepdims=True)
        return exponent / jnp.where(total > 0, total, 1.0)

    own_sent, xn_sent = tie(
        (dot(place_own, xn_second).astype(bf16), xn_second), "grad_rows_far", *coming(turns[2])
    )
    fetch(turns[3], *coming(turns[2]))
    box["received_own"] = exchange(mark(own_sent))
    fetch([0])
    box["in", 0] = mark(tie(box["in", 0], *coming(turns[2])))
    xn_sent = tie(xn_sent, "received_own", *coming(turns[3]))
    box["xn_far"] = swap(xn_sent, "h")
    fetch(near[2], *coming(turns[3]))
    far_sent = tie(dot(place_far, box["xn_far"]).astype(bf16), *coming(near[2]))
    box["received_far"] = exchange(far_sent)
    gate_up_full, down_full = assemble()
    box["own"] = expert_part(
        my_expert, box["received_own"], box["grad_rows_own"], router_weight, gate_up_full, down_full
    )
    xn_far = box["xn_far"]
    gates = gating(xn_second, mask_own)
    gates_far = gating(xn_far, mask_far)

    box["back_in_own"] = exchange(tie(box["own"][4], "received_far"))
    box["far"] = expert_part(
        my_expert, box["received_far"], box["grad_rows_far"], router_weight, gate_up_full, down_full
    )
    box["back_in_far"] = exchange(tie(box["far"][4], "back_in_own"))
    box["d_in_sum_far"] = swap(t_dot(place_far, box["back_in_far"]).astype(bf16), "h")
    received, d_projected, inner, d_out = [
        list(pair)
        for pair in zip(
            (box["received_own"], box["own"][3], box["own"][0], box["own"][2]),
            (box["received_far"], box["far"][3], box["far"][0], box["far"][2]),
        )
    ]
    up_grad, down_grad = expert_weights(received, d_projected, inner, d_out)
    give(stay, up_grad, down_grad)

    d_in_sum = t_dot(place_own, box["back_in_own"])

    def gate_columns(wide):
        high = wide[:, model_width : model_width + half_experts]
        low = wide[:, model_width + half_experts : model_width + 2 * half_experts]
        return high.astype(f32) + low.astype(f32)

    d_in_sum_far = box["d_in_sum_far"]
    d_gates = both_columns(gate_columns(d_in_sum), gate_columns(d_in_sum_far))
    d_in_sum = d_in_sum[:, :model_width] + d_in_sum_far[:, :model_width].astype(f32)
    d_chosen = gates * (d_gates - jnp.sum(gates * d_gates, axis=-1, keepdims=True))
    d_logits = d_chosen.astype(bf16)
    router_local = t_dot(d_logits, xn_second)
    d_xn_second = dot_t(d_logits, router_weight) + d_in_sum

    def mix(cube, gate, back):
        spread = jnp.where(cube, half_columns(gate, half).T[:, None, :], 0.0).reshape(rows, seq_len)
        high = spread.astype(bf16)
        low = (spread - high.astype(f32)).astype(bf16)
        return t_dot(high, back) + t_dot(low, back)

    d_hidden_norm, gain_moe_local = norm_second_pull(d_xn_second)
    d_hidden = grad_f + d_hidden_norm
    d_hidden_b = d_hidden.astype(bf16)
    d_hidden_b, out_far = together(d_hidden_b, box["far"][1])
    box["back_out_far"] = exchange(out_far)
    d_hidden_b, up_grad, down_grad = together(d_hidden_b, up_grad, down_grad)
    give(same, up_grad, down_grad)
    d_attended = dot_t(d_hidden_b, out_full).astype(bf16)

    def halves(value):
        first, last = jnp.split(value, 2, axis=1)
        return jnp.where(core == 0, first, last), jnp.where(core == 0, last, first)

    d_att_mine, d_att_send = halves(d_attended)
    grad_heads = jnp.stack([d_att_mine, swap(d_att_send, "c")]).reshape(2 * seq_len, query_half)
    d_hid_mine, d_hid_send = halves(d_hidden_b)
    d_hid_next = swap(d_hid_send, "c")
    out_pair = (
        jnp.concatenate([attended, attended_next], axis=0),
        jnp.concatenate([d_hid_mine, d_hid_next], axis=0),
    )
    out_sends = scatter_sends(*out_pair)
    grad_heads = mark(grad_heads)
    grad_joint, d_xn_pair = attend_backward(joint, grad_heads, qkv_core, seq_len)
    grad_joint, out_sends, out_own = tie((grad_joint, out_sends, box["own"][1]), "back_out_far")
    box["back_out_own"] = exchange(out_own)
    moe_sent = mix(cube_far, gates_far, box["back_out_far"]).astype(bf16)

    def first_round(blocks):
        blocks, sent = tie((blocks, moe_sent), "small", "back_out_own", *going(same))
        box["moe_far"] = swap(sent, "h")
        give(opposite, up_grad, down_grad, *going(same))
        box["small"] = sum_over(box["small"], ("c", "y", "r"))
        return mark(blocks)

    def second_round(blocks):
        blocks = tie(blocks, "small", "moe_far", *going(opposite))
        give(across + level, up_grad, down_grad, *going(opposite))
        box["small"] = sum_over(box["small"], ("h",))
        return mark(blocks)

    def third_round(blocks):
        return tie(blocks, "small", *going(across + level))

    d_xn_first = d_xn_pair[:seq_len] + swap(d_xn_pair[seq_len:], "c")
    d_token_norm, gain_attn_local = norm_first_pull(d_xn_first)
    grad_tokens = d_hidden + d_token_norm

    box["small"] = jnp.concatenate([router_local, gain_moe_local[None], gain_attn_local[None]], axis=0)
    qkv_grad, out_grad = scatter_products(
        ((xn_pair, grad_joint), out_pair),
        (scatter_sends(xn_pair, grad_joint), out_sends),
        (first_round, second_round, third_round),
    )
    moe_own = mix(cube_own, gates, box["back_out_own"])
    small = box["small"]
    mixed = (hidden + (moe_own + box["moe_far"].astype(f32))).astype(bf16)
    grad_gate_up, grad_down = collect()
    grad_out_proj = order_by(core, out_grad.astype(f32), swap(out_grad, "c").astype(f32), 1)
    qkv_grad_other = swap(qkv_grad, "c")
    first = jnp.where(core == 0, qkv_grad, qkv_grad_other).astype(f32)
    last = jnp.where(core == 0, qkv_grad_other, qkv_grad).astype(f32)
    cut = (query_half, query_half + kv_half)
    grad_qkv = jnp.concatenate(
        [piece for pair in zip(jnp.split(first, cut, axis=1), jnp.split(last, cut, axis=1)) for piece in pair],
        axis=1,
    )

    return (
        mixed,
        grad_tokens,
        small[EXPERTS + 1],
        grad_qkv,
        grad_out_proj,
        small[EXPERTS],
        small[:EXPERTS].T,
        grad_gate_up,
        grad_down,
    )


def solution(mesh):
    expert, fsdp = mesh.devices.shape
    fine = Mesh(mesh.devices.reshape(expert // 2, 2, 2, fsdp // 2), BOTH)
    in_specs = (
        P(BOTH, None),
        P(BOTH, None),
        P(),
        P(FSDP, None),
        P(FSDP, None),
        P(),
        P(),
        P(EXPERT, FSDP, None),
        P(EXPERT, FSDP, None),
        P(BOTH, None),
    )
    out_specs = (
        P(BOTH, None),
        P(BOTH, None),
        P(),
        P(FSDP, None),
        P(FSDP, None),
        P(),
        P(),
        P(EXPERT, FSDP, None),
        P(EXPERT, FSDP, None),
    )
    return jax.shard_map(shards, mesh=fine, in_specs=in_specs, out_specs=out_specs, check_vma=False)
```

```python
import functools

import jax
import jax.numpy as jnp
from jax import lax
from jax.experimental import pallas as pl
from jax.experimental.pallas import tpu as pltpu
from jax.sharding import Mesh
from jax.sharding import PartitionSpec as P

HEADS = 12
KV_HEADS = 2
HEAD_DIM = 128
FFE = 768
EXPERTS = 32
CAP = 48
EPSILON = 1e-06
VMEM_LIMIT = 56 * 1024 * 1024
EXTRA = 128
INWARD = [[(-1, 0), (-2, 0)], [(-3, 0), (0, 1)], [(-2, 1)], [(-3, 1)], [(-1, 1)]]
OUTWARD = [[(1, 0), (3, 0)], [(2, 0)], [(2, 1)], [(1, 1), (3, 1), (0, 1)]]
EXPERT = ("y", "c")
FSDP = ("h", "r")
BOTH = EXPERT + FSDP
HALF = ("y", "c", "r")
f32 = jnp.float32
bf16 = jnp.bfloat16


def dot(a, b):
    return jnp.dot(a, b, preferred_element_type=f32)


def dot_t(a, b):
    return lax.dot_general(a, b, (((1,), (1,)), ((), ())), preferred_element_type=f32)


def t_dot(a, b):
    return lax.dot_general(a, b, (((0,), (0,)), ((), ())), preferred_element_type=f32)


def rms_apply(values, gain):
    return values * lax.rsqrt(jnp.mean(values * values, axis=-1, keepdims=True) + EPSILON) * gain


def swap(value, axis, bit=1):
    size = lax.axis_size(axis)
    return lax.ppermute(value, axis, [(i, i ^ bit) for i in range(size)])


def sum_over(value, axes):
    for axis in axes:
        bit = 1
        while bit < lax.axis_size(axis):
            value = value + swap(value, axis, bit)
            bit *= 2
    return value


def together(*values):
    return lax.optimization_barrier(values)


def marker_kernel(*refs):
    pass


def mark(values):
    flat, tree = jax.tree.flatten(values)
    anywhere = [pl.BlockSpec(memory_space=pl.ANY)] * len(flat)
    same = pl.pallas_call(
        marker_kernel,
        in_specs=anywhere,
        out_specs=anywhere,
        out_shape=[jax.ShapeDtypeStruct(value.shape, value.dtype) for value in flat],
        input_output_aliases={number: number for number in range(len(flat))},
        cost_estimate=pl.CostEstimate(flops=10**12, bytes_accessed=0, transcendentals=0),
    )(*flat)
    return jax.tree.unflatten(tree, same)


def order_by(index, mine, other, axis):
    size = mine.shape[axis]
    shape = mine.shape[:axis] + (2 * size,) + mine.shape[axis + 1 :]
    start = [0] * mine.ndim
    start[axis] = index * size
    both = lax.dynamic_update_slice(jnp.zeros(shape, mine.dtype), mine, start)
    start[axis] = (1 - index) * size
    return lax.dynamic_update_slice(both, other, start)


def part_of(value, index, axis):
    size = value.shape[axis] // 2
    return lax.dynamic_slice_in_dim(value, index * size, size, axis=axis)


def split_width(width):
    first = (width // 2 + 127) // 128 * 128
    return first, width - first


def fsdp_bits():
    size = lax.axis_size("r")
    bits = [("h", 1, 0)]
    bit = size // 2
    while bit:
        bits.append(("r", bit, len(bits)))
        bit //= 2
    return bits


def bit_index(axis, bit):
    return (lax.axis_index(axis) // bit) % 2


def gather_step(block, step):
    axis, bit, dim = step
    return order_by(bit_index(axis, bit), block, swap(block, axis, bit), dim)


def scatter_step(block, step):
    axis, bit, dim = step
    index = bit_index(axis, bit)
    other = swap(part_of(block, 1 - index, dim).astype(bf16), axis, bit)
    return part_of(block, index, dim).astype(f32) + other.astype(f32)


def gather_shards(shard, first_done):
    steps = fsdp_bits()
    rows, columns = shard.shape
    whole_rows = rows * lax.axis_size(FSDP)
    shape = (1,) * len(steps) + (rows, columns)
    if lax.axis_size("y") != 2:
        block = shard.reshape(shape)
        for step in steps:
            block = gather_step(block, step)
        return first_done(block).reshape(whole_rows, columns)
    lane = len(steps) + 1
    y_step, x_step = ("y", 1, lane), steps[-1]
    block = part_of(shard.reshape(shape), lax.axis_index("y"), lane)
    for step in steps[:-1]:
        block = gather_step(block, step)
    block = first_done(block)
    first, last = jnp.split(block, [split_width(columns // 2)[0]], axis=lane)
    first, last = gather_step(first, x_step), gather_step(last, y_step)
    first, last = gather_step(first, y_step), gather_step(last, x_step)
    parts = [
        piece for pair in zip(jnp.split(first, 2, axis=lane), jnp.split(last, 2, axis=lane)) for piece in pair
    ]
    return jnp.concatenate(parts, axis=lane).reshape(whole_rows, columns)


def product_kernel(width, place_ref, left_ref, right_ref, first_sent_ref, first_ref, last_sent_ref, last_ref):
    rows = left_ref.shape[1] // 2
    product = t_dot(left_ref[...], right_ref[...])
    half = product.shape[1] // 2
    lower = place_ref[0] == 0
    mine = jnp.where(lower, product[:, :width], product[:, half : half + width])
    other = jnp.where(lower, product[:, half : half + width], product[:, :width])
    first_ref[...] = mine
    first_sent_ref[...] = other.astype(bf16)
    last = jnp.concatenate([product[:, width:half], product[:, half + width :]], axis=1)
    near = place_ref[1] == 0
    last_ref[...] = jnp.where(near, last[:rows], last[rows:])
    last_sent_ref[...] = jnp.where(near, last[rows:], last[:rows]).astype(bf16)


def scatter_sends(left, right):
    if lax.axis_size("y") != 2:
        return None
    x_step = fsdp_bits()[-1]
    tokens, whole_rows = left.shape
    columns = right.shape[1]
    rows = whole_rows // lax.axis_size(FSDP)
    width = split_width(columns // 2)[0]
    place = jnp.stack([lax.axis_index("y"), bit_index(*x_step[:2])]).astype(jnp.int32)

    def out(count, wide, kind):
        return pl.BlockSpec((count, wide), lambda i, *_: (i, 0)), jax.ShapeDtypeStruct(
            (whole_rows // (2 * rows) * count, wide), kind
        )

    rest = columns - 2 * width
    outs = [out(2 * rows, width, bf16), out(2 * rows, width, f32), out(rows, rest, bf16), out(rows, rest, f32)]
    first_sent, first, last_sent, last = pl.pallas_call(
        functools.partial(product_kernel, width),
        grid_spec=pltpu.PrefetchScalarGridSpec(
            num_scalar_prefetch=1,
            grid=(whole_rows // (2 * rows),),
            in_specs=[
                pl.BlockSpec((tokens, 2 * rows), lambda i, *_: (0, i)),
                pl.BlockSpec((tokens, columns), lambda i, *_: (0, 0)),
            ],
            out_specs=[spec for spec, _ in outs],
        ),
        out_shape=[shape for _, shape in outs],
        compiler_params=pltpu.CompilerParams(vmem_limit_bytes=VMEM_LIMIT),
        cost_estimate=pl.CostEstimate(flops=0, bytes_accessed=0, transcendentals=0),
    )(place, left, right)
    return first, swap(first_sent, "y"), last, swap(last_sent, *x_step[:2])


def scatter_products(pairs, sends, rounds):
    steps = fsdp_bits()
    size = lax.axis_size(FSDP)
    if lax.axis_size("y") != 2:
        blocks = [t_dot(left, right) for left, right in pairs]
        blocks = [block.reshape((2,) * len(steps) + (block.shape[0] // size, -1)) for block in blocks]
        for number, step in enumerate(reversed(steps)):
            blocks = [scatter_step(block, step) for block in blocks]
            if number < 2:
                blocks = rounds[number](blocks)
        blocks = rounds[2](blocks)
        blocks = [block.astype(bf16).reshape(block.shape[-2:]) for block in blocks]
        return [sum_over(block, ("y",)).astype(bf16) for block in blocks]
    lane = len(steps) + 1
    y_step, x_step = ("y", 1, lane), steps[-1]
    y_index, x_index = lax.axis_index("y"), bit_index(*x_step[:2])
    firsts, lasts = [], []
    for first, first_sent, last, last_sent in sends:
        rows = first.shape[0] // size
        first = first + first_sent.astype(f32)
        last = last + last_sent.astype(f32)
        firsts.append(first.reshape((2,) * len(steps) + (rows, -1)))
        lasts.append(last.reshape((2,) * (len(steps) - 1) + (1, rows, 2, last.shape[1] // 2)))
    widths = [block.shape[-1] for block in firsts + lasts]
    first = jnp.concatenate(firsts, axis=lane)
    last = jnp.concatenate(lasts, axis=lane + 1)
    last = last.reshape(last.shape[:lane] + (-1,))
    first, last = rounds[0]((first, last))
    first, last = scatter_step(first, x_step), scatter_step(last, y_step)
    block = rounds[1](jnp.concatenate([first, last], axis=lane))
    for step in reversed(steps[:-1]):
        block = scatter_step(block, step)
    block = rounds[2](block).astype(bf16).reshape(block.shape[-2:])
    cuts = [sum(widths[: number + 1]) for number in range(len(widths) - 1)]
    halves = [jnp.split(half, cuts, axis=1) for half in jnp.split(order_by(y_index, block, swap(block, "y"), 1), 2, axis=1)]
    count = len(pairs)
    return [
        jnp.concatenate([half[number + part] for half in halves for part in (0, count)], axis=1)
        for number in range(count)
    ]


def head_probs(query, key):
    seq_len = query.shape[0]
    scores = dot_t(query, key) * HEAD_DIM ** (-0.5)
    rows = lax.broadcasted_iota(jnp.int32, (seq_len, seq_len), 0)
    columns = lax.broadcasted_iota(jnp.int32, (seq_len, seq_len), 1)
    scores = jnp.where(rows >= columns, scores, -1e30)
    exponent = jnp.exp(scores - jnp.max(scores, axis=-1, keepdims=True))
    return exponent / jnp.sum(exponent, axis=-1, keepdims=True)


def attend_kernel(xn_ref, weight_ref, joint_ref, attended_ref):
    joint = dot(xn_ref[...], weight_ref[...]).astype(bf16)
    joint_ref[...] = joint
    width = HEADS // 2 * HEAD_DIM
    key, value = joint[:, width : width + HEAD_DIM], joint[:, width + HEAD_DIM :]
    for head in range(HEADS // 2):
        columns = slice(head * HEAD_DIM, (head + 1) * HEAD_DIM)
        probs = head_probs(joint[:, columns], key).astype(bf16)
        attended_ref[:, columns] = dot(probs, value).astype(bf16)


def attend(xn_pair, weight, seq_len):
    rows, model_width = xn_pair.shape
    width = weight.shape[1]
    query_width = HEADS // 2 * HEAD_DIM
    return pl.pallas_call(
        attend_kernel,
        grid=(rows // seq_len,),
        in_specs=[
            pl.BlockSpec((seq_len, model_width), lambda i: (i, 0)),
            pl.BlockSpec((model_width, width), lambda i: (0, 0)),
        ],
        out_specs=[
            pl.BlockSpec((seq_len, width), lambda i: (i, 0)),
            pl.BlockSpec((seq_len, query_width), lambda i: (i, 0)),
        ],
        out_shape=[
            jax.ShapeDtypeStruct((rows, width), bf16),
            jax.ShapeDtypeStruct((rows, query_width), bf16),
        ],
        compiler_params=pltpu.CompilerParams(vmem_limit_bytes=VMEM_LIMIT),
        cost_estimate=pl.CostEstimate(flops=0, bytes_accessed=0, transcendentals=0),
    )(xn_pair, weight)


def attend_backward_kernel(joint_ref, grad_ref, weight_ref, grad_joint_ref, grad_xn_ref):
    scale = HEAD_DIM ** (-0.5)
    width = HEADS // 2 * HEAD_DIM
    joint = joint_ref[...]
    grad = grad_ref[...]
    key, value = joint[:, width : width + HEAD_DIM], joint[:, width + HEAD_DIM :]
    grad_key = jnp.zeros(key.shape, f32)
    grad_value = jnp.zeros(value.shape, f32)
    for head in range(HEADS // 2):
        columns = slice(head * HEAD_DIM, (head + 1) * HEAD_DIM)
        query, grad_head = joint[:, columns], grad[:, columns]
        probs = head_probs(query, key)
        grad_probs = dot_t(grad_head, value)
        delta = jnp.sum(probs * grad_probs, axis=-1, keepdims=True)
        grad_scores = (probs * (grad_probs - delta)).astype(bf16)
        grad_joint_ref[:, columns] = (dot(grad_scores, key) * scale).astype(bf16)
        grad_key = grad_key + t_dot(grad_scores, query)
        grad_value = grad_value + t_dot(probs.astype(bf16), grad_head)
    grad_joint_ref[:, width : width + HEAD_DIM] = (grad_key * scale).astype(bf16)
    grad_joint_ref[:, width + HEAD_DIM :] = grad_value.astype(bf16)
    grad_xn_ref[...] = dot_t(grad_joint_ref[...], weight_ref[...])


def attend_backward(joint, grad_attended, weight, seq_len):
    rows, width = joint.shape
    model_width = weight.shape[0]
    query_width = HEADS // 2 * HEAD_DIM
    return pl.pallas_call(
        attend_backward_kernel,
        grid=(rows // seq_len,),
        in_specs=[
            pl.BlockSpec((seq_len, width), lambda i: (i, 0)),
            pl.BlockSpec((seq_len, query_width), lambda i: (i, 0)),
            pl.BlockSpec((model_width, width), lambda i: (0, 0)),
        ],
        out_specs=[
            pl.BlockSpec((seq_len, width), lambda i: (i, 0)),
            pl.BlockSpec((seq_len, model_width), lambda i: (i, 0)),
        ],
        out_shape=[
            jax.ShapeDtypeStruct((rows, width), bf16),
            jax.ShapeDtypeStruct((rows, model_width), f32),
        ],
        compiler_params=pltpu.CompilerParams(vmem_limit_bytes=VMEM_LIMIT),
        cost_estimate=pl.CostEstimate(flops=0, bytes_accessed=0, transcendentals=0),
    )(joint, grad_attended, weight)


def expert_kernel(
    expert_ref,
    rows_ref,
    grad_ref,
    router_ref,
    up_ref,
    down_ref,
    inner_ref,
    out_ref,
    d_out_ref,
    d_projected_ref,
    d_in_ref,
):
    rows = rows_ref[...]
    width = rows.shape[1]
    mask = grad_ref[:, width : width + EXPERTS] > 0
    logits = jnp.where(mask, dot(rows, router_ref[...]), -1e30)
    exponent = jnp.where(mask, jnp.exp(logits - jnp.max(logits, axis=-1, keepdims=True)), 0.0)
    total = jnp.sum(exponent, axis=-1, keepdims=True)
    mine = lax.broadcasted_iota(jnp.int32, exponent.shape, 1) == expert_ref[0]
    gate = jnp.sum(jnp.where(mine, exponent, 0.0), axis=-1, keepdims=True)
    gate = gate / jnp.where(total > 0, total, 1.0)

    projected = dot(rows, up_ref[...])
    lower, upper = projected[:, :FFE], projected[:, FFE:]
    slope = (2.0 / 3.141592653589793) ** 0.5
    bend = jnp.tanh(slope * (lower + 0.044715 * lower * lower * lower))
    gelu = 0.5 * lower * (1.0 + bend)
    gelu_grad = 0.5 * (1.0 + bend) + 0.5 * lower * (1.0 - bend * bend) * slope * (
        1.0 + 3 * 0.044715 * lower * lower
    )
    inner = (gelu * upper).astype(bf16)
    inner_ref[...] = inner
    out = dot(inner, down_ref[...]).astype(bf16)
    out_ref[...] = out
    grad = grad_ref[:, :width].astype(f32)
    d_gate = jnp.sum(out.astype(f32) * grad, axis=-1, keepdims=True)
    d_gate_high = d_gate.astype(bf16).astype(f32)
    column = lax.broadcasted_iota(jnp.int32, (rows.shape[0], EXTRA), 1)
    d_in_ref[:, width:] = jnp.where(
        column == expert_ref[1],
        d_gate_high,
        jnp.where(column == expert_ref[1] + EXPERTS // 2, d_gate - d_gate_high, 0.0),
    ).astype(bf16)
    d_out = (gate * grad).astype(bf16)
    d_out_ref[...] = d_out
    d_inner = dot_t(d_out, down_ref[...])
    d_projected_ref[:, :FFE] = (d_inner * upper * gelu_grad).astype(bf16)
    d_projected_ref[:, FFE:] = (d_inner * gelu).astype(bf16)
    d_in_ref[:, :width] = dot_t(d_projected_ref[...], up_ref[...]).astype(bf16)


def expert_part(expert, received, grad_rows, router, up, down):
    rows, model_width = received.shape
    block = 256

    def row_block(width):
        return pl.BlockSpec((block, width), lambda i, *_: (i, 0))

    def whole(array):
        return pl.BlockSpec(array.shape, lambda i, *_: (0, 0))

    widths = (FFE, model_width, model_width, 2 * FFE, model_width + EXTRA)
    return pl.pallas_call(
        expert_kernel,
        grid_spec=pltpu.PrefetchScalarGridSpec(
            num_scalar_prefetch=1,
            grid=(rows // block,),
            in_specs=[
                row_block(model_width),
                row_block(model_width + EXTRA),
                whole(router),
                whole(up),
                whole(down),
            ],
            out_specs=[row_block(width) for width in widths],
        ),
        out_shape=[jax.ShapeDtypeStruct((rows, width), bf16) for width in widths],
        compiler_params=pltpu.CompilerParams(vmem_limit_bytes=VMEM_LIMIT),
        cost_estimate=pl.CostEstimate(flops=0, bytes_accessed=0, transcendentals=0),
    )(expert, received, grad_rows, router, up, down)


def token_backward_kernel(
    core_ref,
    place_ref,
    back_ref,
    far_ref,
    spread_ref,
    gates_ref,
    router_ref,
    xn_ref,
    hidden_ref,
    gain_ref,
    grad_ref,
    weight_ref,
    d_hidden_ref,
    d_hidden_b_ref,
    d_attended_ref,
    small_ref,
):
    width = hidden_ref.shape[1]
    part = EXPERTS // 2
    wide = t_dot(place_ref[...], back_ref[...])
    far = far_ref[...]
    d_gates = jnp.zeros(gates_ref.shape, f32)
    for number, extra in enumerate((wide[:, width:].astype(bf16), far[:, width:])):
        for start in (0, part):
            d_gates = d_gates + dot(extra[:, start : start + part], spread_ref[number])
    gates = gates_ref[...]
    d_chosen = gates * (d_gates - jnp.sum(gates * d_gates, axis=-1, keepdims=True))
    d_logits = d_chosen.astype(bf16)
    d_xn = dot_t(d_logits, router_ref[...]) + wide[:, :width] + far[:, :width].astype(f32)
    hidden = hidden_ref[...]
    scale = lax.rsqrt(jnp.mean(hidden * hidden, axis=-1, keepdims=True) + EPSILON)
    normed = hidden * scale
    scaled = d_xn * gain_ref[...]
    d_hidden = grad_ref[...].astype(f32) + scale * (
        scaled - normed * jnp.mean(scaled * normed, axis=-1, keepdims=True)
    )
    d_hidden_ref[...] = d_hidden
    d_hidden_b = d_hidden.astype(bf16)
    d_hidden_b_ref[...] = d_hidden_b
    small_ref[:EXPERTS] = t_dot(d_logits, xn_ref[...])
    small_ref[EXPERTS:] = jnp.broadcast_to(jnp.sum(d_xn * normed, axis=0, keepdims=True), (8, width))
    d_attended = dot_t(d_hidden_b, weight_ref[...]).astype(bf16)
    first, last = d_attended[:, : width // 2], d_attended[:, width // 2 :]
    lower = core_ref[0] == 0
    d_attended_ref[0] = jnp.where(lower, first, last)
    d_attended_ref[1] = jnp.where(lower, last, first)


def token_backward(core, place, back, far, spread, gates, router, xn, hidden, gain, grad, weight):
    seq_len, width = hidden.shape
    return pl.pallas_call(
        token_backward_kernel,
        in_specs=[pl.BlockSpec(memory_space=pltpu.SMEM)] + [pl.BlockSpec(memory_space=pltpu.VMEM)] * 11,
        out_specs=[pl.BlockSpec(memory_space=pltpu.VMEM)] * 4,
        out_shape=[
            jax.ShapeDtypeStruct((seq_len, width), f32),
            jax.ShapeDtypeStruct((seq_len, width), bf16),
            jax.ShapeDtypeStruct((2, seq_len, width // 2), bf16),
            jax.ShapeDtypeStruct((EXPERTS + 8, width), f32),
        ],
        compiler_params=pltpu.CompilerParams(vmem_limit_bytes=VMEM_LIMIT),
        cost_estimate=pl.CostEstimate(flops=0, bytes_accessed=0, transcendentals=0),
    )(core, place, back, far, spread, gates, router, xn, hidden, gain, grad, weight)


def expert_weights_kernel(x_own, x_far, p_own, p_far, i_own, i_far, d_own, d_far, up_ref, down_ref):
    up_ref[...] = (t_dot(x_own[...], p_own[...]) + t_dot(x_far[...], p_far[...])).astype(bf16)
    down_ref[...] = (t_dot(i_own[...], d_own[...]) + t_dot(i_far[...], d_far[...])).astype(bf16)


def expert_weights(received, d_projected, inner, d_out):
    rows, model_width = received[0].shape
    steps = 3

    def columns(array):
        return pl.BlockSpec((rows, array.shape[1] // steps), lambda i: (0, i))

    def whole(array):
        return pl.BlockSpec(array.shape, lambda i: (0, 0))

    return pl.pallas_call(
        expert_weights_kernel,
        grid=(steps,),
        in_specs=[columns(a) for a in received]
        + [whole(a) for a in d_projected]
        + [columns(a) for a in inner]
        + [whole(a) for a in d_out],
        out_specs=[
            pl.BlockSpec((model_width // steps, 2 * FFE), lambda i: (i, 0)),
            pl.BlockSpec((FFE // steps, model_width), lambda i: (i, 0)),
        ],
        out_shape=[
            jax.ShapeDtypeStruct((model_width, 2 * FFE), bf16),
            jax.ShapeDtypeStruct((FFE, model_width), bf16),
        ],
        compiler_params=pltpu.CompilerParams(vmem_limit_bytes=VMEM_LIMIT),
        cost_estimate=pl.CostEstimate(flops=0, bytes_accessed=0, transcendentals=0),
    )(*received, *d_projected, *inner, *d_out)


def shards(
    tokens,
    routes,
    norm_attn,
    qkv_weight,
    out_weight,
    norm_moe,
    router_weight,
    gate_up,
    down,
    grad_output,
):
    seq_len, model_width = tokens.shape
    query_half = HEADS * HEAD_DIM // 2
    kv_half = KV_HEADS * HEAD_DIM // 2
    out_half = out_weight.shape[1] // 2
    groups = lax.axis_size(EXPERT)
    fsdp = lax.axis_size(FSDP)
    half_devices = groups * fsdp // 2
    local_count = gate_up.shape[0]
    parts = fsdp // local_count
    half_experts = EXPERTS // 2
    rows = half_experts * CAP
    core = lax.axis_index("c")
    half = lax.axis_index("h")
    me = lax.axis_index(FSDP)
    group = lax.axis_index(EXPERT)
    my_expert = jnp.stack(
        [
            group * local_count + me // parts,
            group * (local_count // 2) + me // parts - half * (local_count // 2),
        ]
    ).astype(jnp.int32)

    box = {}

    def tie(value, *names):
        value, held = together(value, [box[name] for name in names])
        box.update(zip(names, held))
        return value

    up_width, down_width = gate_up.shape[1], down.shape[1]
    columns = fsdp // 4

    def target(index, move, sign=1):
        step, cross = move
        line = index // columns
        line = (line + sign * step + 4) % 4 if step >= 0 else line ^ -step
        return line * columns + (index % columns ^ cross)

    def every(moves):
        return [
            (step, other) for step, cross in moves for other in (range(1, columns) if cross else range(1))
        ]

    def fetch(moves, *names):
        for move in every(moves):
            expert = target(me, move) // parts
            piece = jnp.concatenate(
                [
                    lax.dynamic_index_in_dim(gate_up, expert, 0, keepdims=False),
                    lax.dynamic_index_in_dim(down, expert, 0, keepdims=False),
                ],
                axis=0,
            )
            if move != (0, 0):
                piece = lax.ppermute(tie(piece, *names), FSDP, [(i, target(i, move)) for i in range(fsdp)])
            box["in", move] = piece

    def coming(moves):
        return [("in", move) for move in every(moves)]

    def assemble():
        up_full = jnp.zeros((fsdp * up_width, gate_up.shape[2]), gate_up.dtype)
        down_full = jnp.zeros((fsdp * down_width, down.shape[2]), down.dtype)
        for move in every(sum(INWARD, [(0, 0)])):
            source, piece = target(me, move, -1), box["in", move]
            up_full = lax.dynamic_update_slice(up_full, piece[:up_width], (source * up_width, 0))
            down_full = lax.dynamic_update_slice(down_full, piece[up_width:], (source * down_width, 0))
        return up_full, down_full

    def give(moves, up_grad, down_grad, *names):
        for move in every(moves):
            to = target(me, move)
            piece = jnp.concatenate(
                [
                    lax.dynamic_slice_in_dim(up_grad, to * up_width, up_width, axis=0),
                    lax.dynamic_slice_in_dim(down_grad, to * down_width, down_width, axis=0),
                ],
                axis=0,
            )
            if move != (0, 0):
                piece = lax.ppermute(tie(piece, *names), FSDP, [(i, target(i, move)) for i in range(fsdp)])
            box["out", move] = piece

    def going(moves):
        return [("out", move) for move in every(moves)]

    def collect():
        up_sum = jnp.zeros(gate_up.shape, f32)
        down_sum = jnp.zeros(down.shape, f32)
        for move in every(sum(OUTWARD, [(0, 0)])):
            expert = target(me, move, -1) // parts
            piece = box["out", move].astype(f32)[None]
            up_part, down_part = piece[:, :up_width], piece[:, up_width:]
            if parts > 1:
                up_part = up_part + lax.dynamic_slice_in_dim(up_sum, expert, 1, axis=0)
                down_part = down_part + lax.dynamic_slice_in_dim(down_sum, expert, 1, axis=0)
            up_sum = lax.dynamic_update_slice(up_sum, up_part, (expert, 0, 0))
            down_sum = lax.dynamic_update_slice(down_sum, down_part, (expert, 0, 0))
        return up_sum, down_sum

    def exchange(buffer):
        shape = buffer.shape
        return lax.all_to_all(
            buffer.reshape((half_devices, rows // half_devices) + shape[1:]),
            HALF,
            split_axis=0,
            concat_axis=0,
            tiled=True,
        ).reshape(shape)

    def half_columns(table, index):
        cube = table.reshape(table.shape[0], groups, 2, local_count // 2)
        return lax.dynamic_index_in_dim(cube, index, 2, keepdims=False).reshape(table.shape[0], half_experts)

    token_f = tokens.astype(f32)

    qkv_mine = jnp.concatenate(
        [
            lax.dynamic_slice_in_dim(qkv_weight, core * query_half, query_half, axis=1),
            lax.dynamic_slice_in_dim(qkv_weight, 2 * query_half + core * kv_half, kv_half, axis=1),
            lax.dynamic_slice_in_dim(qkv_weight, 2 * query_half + (2 + core) * kv_half, kv_half, axis=1),
        ],
        axis=1,
    )
    out_mine = lax.dynamic_slice_in_dim(out_weight, core * out_half, out_half, axis=1)
    expert_ids = jnp.arange(EXPERTS, dtype=jnp.int32)
    order = jnp.arange(seq_len)
    earlier = (order[None, :] < order[:, None]).astype(bf16)

    def placing(routing):
        mask = jnp.any(routing[:, :, None] == expert_ids[None, None, :], axis=1)
        position = dot(earlier, mask.astype(bf16)).astype(jnp.int32)
        slot = half_columns(jnp.where(mask, position, -1), half).T
        place = slot[:, None, :] == jnp.arange(CAP, dtype=jnp.int32)[None, :, None]
        return mask, place

    mask_own, cube_own = placing(routes)
    mask_far, cube_far = placing(swap(routes, "h"))
    place_own = cube_own.astype(bf16).reshape(rows, seq_len)
    place_far = cube_far.astype(bf16).reshape(rows, seq_len)

    def first_done(block):
        nonlocal gate_up, down
        sent, block, gate_up, down = together(grad_output, block, gate_up, down)
        box["grad_far"] = swap(sent, "h")
        fetch(INWARD[0])
        return mark(block)

    def send_rows(place, grad, mask):
        extra = jnp.pad(mask.astype(bf16), ((0, 0), (0, EXTRA - EXPERTS)))
        return dot(place, jnp.concatenate([grad, extra], axis=1)).astype(bf16)

    xn_first_f, norm_first_pull = jax.vjp(rms_apply, token_f, norm_attn)
    xn_first = xn_first_f.astype(bf16)
    xn_pair = jnp.concatenate([xn_first, swap(xn_first, "c")], axis=0)
    shard = jnp.concatenate([qkv_mine, out_mine], axis=1)
    core_weights, xn_pair, own_sent = tie(
        (gather_shards(shard, first_done), xn_pair, send_rows(place_own, grad_output, mask_own)),
        "grad_far",
        *coming(INWARD[0]),
    )
    fetch(INWARD[1], *coming(INWARD[0]))
    box["grad_rows_own"] = exchange(own_sent)
    xn_pair = mark(xn_pair)
    qkv_width = query_half + 2 * kv_half
    qkv_core, out_core = core_weights[:, :qkv_width], core_weights[:, qkv_width:]

    joint, attended_mine = attend(xn_pair, qkv_core, seq_len)
    out_full = order_by(core, out_core, swap(out_core, "c"), 1)
    attended_mine = attended_mine.reshape(2, seq_len, query_half)
    far_sent = send_rows(place_far, box["grad_far"], mask_far)
    attended_mine, far_sent = tie((attended_mine, far_sent), "grad_rows_own", *coming(INWARD[1]))
    fetch(INWARD[2], *coming(INWARD[1]))
    box["grad_rows_far"] = exchange(far_sent)
    attended_mine = mark(attended_mine)
    attended_other = swap(attended_mine, "c")
    attended = order_by(core, attended_mine[0], attended_other[1], 1)
    attended_next = order_by(core, attended_mine[1], attended_other[0], 1)
    hidden = token_f + dot(attended, out_full)
    xn_second = rms_apply(hidden, norm_moe).astype(bf16)

    def gating(values_b, mask):
        logits = dot(values_b, router_weight)
        top = jnp.max(jnp.where(mask, logits, -1e30), axis=-1, keepdims=True)
        exponent = jnp.where(mask, jnp.exp(jnp.where(mask, logits - top, 0.0)), 0.0)
        total = jnp.sum(exponent, axis=-1, keepdims=True)
        return exponent / jnp.where(total > 0, total, 1.0)

    own_sent, xn_sent = tie(
        (dot(place_own, xn_second).astype(bf16), xn_second), "grad_rows_far", *coming(INWARD[2])
    )
    fetch(INWARD[3], *coming(INWARD[2]))
    box["received_own"] = exchange(mark(own_sent))
    fetch([(0, 0)])
    box["in", (0, 0)] = mark(tie(box["in", (0, 0)], *coming(INWARD[2])))
    xn_sent = tie(xn_sent, "received_own", *coming(INWARD[3]))
    box["xn_far"] = swap(xn_sent, "h")
    fetch(INWARD[4], *coming(INWARD[3]))
    far_sent = tie(dot(place_far, box["xn_far"]).astype(bf16), *coming(INWARD[4]))
    box["received_far"] = exchange(far_sent)
    gate_up_full, down_full = assemble()
    box["own"] = expert_part(
        my_expert, box["received_own"], box["grad_rows_own"], router_weight, gate_up_full, down_full
    )
    xn_far = box["xn_far"]
    gates = gating(xn_second, mask_own)
    gates_far = gating(xn_far, mask_far)

    box["back_in_own"] = exchange(tie(box["own"][4], "received_far"))
    box["far"] = expert_part(
        my_expert, box["received_far"], box["grad_rows_far"], router_weight, gate_up_full, down_full
    )
    received, d_projected, inner, d_out = [
        list(pair)
        for pair in zip(
            (box["received_own"], box["own"][3], box["own"][0], box["own"][2]),
            (box["received_far"], box["far"][3], box["far"][0], box["far"][2]),
        )
    ]
    up_grad, down_grad = expert_weights(received, d_projected, inner, d_out)
    sent, up_grad, down_grad = tie((box["far"][4], up_grad, down_grad), "back_in_own")
    box["back_in_far"] = exchange(sent)
    give(OUTWARD[0], up_grad, down_grad)
    box["d_in_sum_far"] = swap(t_dot(place_far, box["back_in_far"]).astype(bf16), "h")
    give([(0, 0)], up_grad, down_grad)

    places = jnp.arange(EXPERTS) // local_count * (local_count // 2) + jnp.arange(EXPERTS) % (local_count // 2)
    side = jnp.arange(EXPERTS) % local_count // (local_count // 2)
    mine = (places[None, :] == jnp.arange(half_experts)[:, None]).astype(bf16)
    spread = jnp.stack([mine * (side == half), mine * (side != half)]).astype(bf16)
    d_hidden, d_hidden_b, d_attended, router_moe = token_backward(
        core.reshape(1).astype(jnp.int32),
        place_own,
        box["back_in_own"],
        box["d_in_sum_far"],
        spread,
        gates,
        router_weight,
        xn_second,
        hidden,
        norm_moe[None],
        grad_output,
        out_full,
    )

    def mix(cube, gate, back):
        spread = jnp.where(cube, half_columns(gate, half).T[:, None, :], 0.0).reshape(rows, seq_len)
        high = spread.astype(bf16)
        low = (spread - high.astype(f32)).astype(bf16)
        return t_dot(high, back) + t_dot(low, back)

    d_hidden_b, up_grad, down_grad, out_far = together(d_hidden_b, up_grad, down_grad, box["far"][1])
    give(OUTWARD[1], up_grad, down_grad)
    box["back_out_far"] = exchange(out_far)

    def halves(value):
        first, last = jnp.split(value, 2, axis=1)
        return jnp.where(core == 0, first, last), jnp.where(core == 0, last, first)

    grad_heads = jnp.stack([d_attended[0], swap(d_attended[1], "c")]).reshape(2 * seq_len, query_half)
    d_hid_mine, d_hid_send = halves(d_hidden_b)
    d_hid_next = swap(d_hid_send, "c")
    out_pair = (
        jnp.concatenate([attended, attended_next], axis=0),
        jnp.concatenate([d_hid_mine, d_hid_next], axis=0),
    )
    out_sends = scatter_sends(*out_pair)
    grad_heads = mark(grad_heads)
    grad_joint, d_xn_pair = attend_backward(joint, grad_heads, qkv_core, seq_len)
    grad_joint, out_own = tie((grad_joint, box["own"][1]), "back_out_far")
    box["back_out_own"] = exchange(out_own)
    moe_sent = mix(cube_far, gates_far, box["back_out_far"]).astype(bf16)

    def first_round(blocks):
        blocks, sent, box["small"] = tie((blocks, moe_sent, box["small"]), *going(OUTWARD[0] + OUTWARD[1]))
        give(OUTWARD[2], up_grad, down_grad)
        box["moe_far"] = swap(sent, "h")
        box["small"] = sum_over(box["small"], ("c", "y", "r", "h"))
        return blocks

    def second_round(blocks):
        blocks = tie(blocks, "moe_far", *going(OUTWARD[2]))
        give(OUTWARD[3], up_grad, down_grad, *going(OUTWARD[2]))
        return blocks

    def third_round(blocks):
        return tie(blocks, *going(OUTWARD[3]))

    d_xn_first = d_xn_pair[:seq_len] + swap(d_xn_pair[seq_len:], "c")
    d_token_norm, gain_attn_local = norm_first_pull(d_xn_first)
    grad_tokens = d_hidden + d_token_norm

    box["small"] = jnp.concatenate([router_moe[: EXPERTS + 1], gain_attn_local[None]], axis=0)
    qkv_grad, out_grad = scatter_products(
        ((xn_pair, grad_joint), out_pair),
        (scatter_sends(xn_pair, grad_joint), out_sends),
        (first_round, second_round, third_round),
    )
    moe_own = mix(cube_own, gates, box["back_out_own"])
    small = box["small"]
    mixed = (hidden + (moe_own + box["moe_far"].astype(f32))).astype(bf16)
    grad_gate_up, grad_down = collect()
    grad_out_proj = order_by(core, out_grad.astype(f32), swap(out_grad, "c").astype(f32), 1)
    qkv_grad_other = swap(qkv_grad, "c")
    first = jnp.where(core == 0, qkv_grad, qkv_grad_other).astype(f32)
    last = jnp.where(core == 0, qkv_grad_other, qkv_grad).astype(f32)
    cut = (query_half, query_half + kv_half)
    grad_qkv = jnp.concatenate(
        [piece for pair in zip(jnp.split(first, cut, axis=1), jnp.split(last, cut, axis=1)) for piece in pair],
        axis=1,
    )

    return (
        mixed,
        grad_tokens,
        small[EXPERTS + 1],
        grad_qkv,
        grad_out_proj,
        small[EXPERTS],
        small[:EXPERTS].T,
        grad_gate_up,
        grad_down,
    )


def solution(mesh):
    expert, fsdp = mesh.devices.shape
    fine = Mesh(mesh.devices.reshape(expert // 2, 2, 2, fsdp // 2), BOTH)
    in_specs = (
        P(BOTH, None),
        P(BOTH, None),
        P(),
        P(FSDP, None),
        P(FSDP, None),
        P(),
        P(),
        P(EXPERT, FSDP, None),
        P(EXPERT, FSDP, None),
        P(BOTH, None),
    )
    out_specs = (
        P(BOTH, None),
        P(BOTH, None),
        P(),
        P(FSDP, None),
        P(FSDP, None),
        P(),
        P(),
        P(EXPERT, FSDP, None),
        P(EXPERT, FSDP, None),
    )
    return jax.shard_map(shards, mesh=fine, in_specs=in_specs, out_specs=out_specs, check_vma=False)
```

```python
import functools

import jax
import jax.numpy as jnp
from jax import lax
from jax.experimental import pallas as pl
from jax.experimental.pallas import tpu as pltpu
from jax.sharding import Mesh
from jax.sharding import PartitionSpec as P

HEADS = 12
KV_HEADS = 2
HEAD_DIM = 128
FFE = 768
EXPERTS = 32
CAP = 48
EPSILON = 1e-06
VMEM_LIMIT = 56 * 1024 * 1024
EXTRA = 128
INWARD = [[(-1, 0), (-2, 0)], [(-3, 0), (0, 1)], [(-2, 1)], [(-3, 1)], [(-1, 1)]]
OUTWARD = [[(1, 0)], [(3, 0), (2, 0)], [(2, 1)], [(1, 1), (3, 1), (0, 1)]]
EXPERT = ("y", "c")
FSDP = ("h", "r")
BOTH = EXPERT + FSDP
HALF = ("y", "c", "r")
f32 = jnp.float32
bf16 = jnp.bfloat16


def dot(a, b):
    return jnp.dot(a, b, preferred_element_type=f32)


def dot_t(a, b):
    return lax.dot_general(a, b, (((1,), (1,)), ((), ())), preferred_element_type=f32)


def t_dot(a, b):
    return lax.dot_general(a, b, (((0,), (0,)), ((), ())), preferred_element_type=f32)


def rms_apply(values, gain):
    return values * lax.rsqrt(jnp.mean(values * values, axis=-1, keepdims=True) + EPSILON) * gain


def swap(value, axis, bit=1):
    size = lax.axis_size(axis)
    return lax.ppermute(value, axis, [(i, i ^ bit) for i in range(size)])


def sum_over(value, axes):
    for axis in axes:
        bit = 1
        while bit < lax.axis_size(axis):
            value = value + swap(value, axis, bit)
            bit *= 2
    return value


def together(*values):
    return lax.optimization_barrier(values)


def marker_kernel(*refs):
    pass


def mark(values):
    flat, tree = jax.tree.flatten(values)
    anywhere = [pl.BlockSpec(memory_space=pl.ANY)] * len(flat)
    same = pl.pallas_call(
        marker_kernel,
        in_specs=anywhere,
        out_specs=anywhere,
        out_shape=[jax.ShapeDtypeStruct(value.shape, value.dtype) for value in flat],
        input_output_aliases={number: number for number in range(len(flat))},
        cost_estimate=pl.CostEstimate(flops=10**12, bytes_accessed=0, transcendentals=0),
    )(*flat)
    return jax.tree.unflatten(tree, same)


def order_by(index, mine, other, axis):
    size = mine.shape[axis]
    shape = mine.shape[:axis] + (2 * size,) + mine.shape[axis + 1 :]
    start = [0] * mine.ndim
    start[axis] = index * size
    both = lax.dynamic_update_slice(jnp.zeros(shape, mine.dtype), mine, start)
    start[axis] = (1 - index) * size
    return lax.dynamic_update_slice(both, other, start)


def part_of(value, index, axis):
    size = value.shape[axis] // 2
    return lax.dynamic_slice_in_dim(value, index * size, size, axis=axis)


def split_width(width):
    first = (width // 2 + 127) // 128 * 128
    return first, width - first


def fsdp_bits():
    size = lax.axis_size("r")
    bits = [("h", 1, 0)]
    bit = size // 2
    while bit:
        bits.append(("r", bit, len(bits)))
        bit //= 2
    return bits


def bit_index(axis, bit):
    return (lax.axis_index(axis) // bit) % 2


def gather_step(block, step):
    axis, bit, dim = step
    return order_by(bit_index(axis, bit), block, swap(block, axis, bit), dim)


def scatter_step(block, step):
    axis, bit, dim = step
    index = bit_index(axis, bit)
    other = swap(part_of(block, 1 - index, dim).astype(bf16), axis, bit)
    return part_of(block, index, dim).astype(f32) + other.astype(f32)


def gather_shards(shard, first_done):
    steps = fsdp_bits()
    rows, columns = shard.shape
    whole_rows = rows * lax.axis_size(FSDP)
    shape = (1,) * len(steps) + (rows, columns)
    if lax.axis_size("y") != 2:
        block = shard.reshape(shape)
        for step in steps:
            block = gather_step(block, step)
        return first_done(block).reshape(whole_rows, columns)
    lane = len(steps) + 1
    y_step, x_step = ("y", 1, lane), steps[-1]
    block = part_of(shard.reshape(shape), lax.axis_index("y"), lane)
    for step in steps[:-1]:
        block = gather_step(block, step)
    block = first_done(block)
    first, last = jnp.split(block, [split_width(columns // 2)[0]], axis=lane)
    first, last = gather_step(first, x_step), gather_step(last, y_step)
    first, last = gather_step(first, y_step), gather_step(last, x_step)
    parts = [
        piece for pair in zip(jnp.split(first, 2, axis=lane), jnp.split(last, 2, axis=lane)) for piece in pair
    ]
    return jnp.concatenate(parts, axis=lane).reshape(whole_rows, columns)


def product_kernel(width, place_ref, left_ref, right_ref, first_sent_ref, first_ref, last_sent_ref, last_ref):
    rows = left_ref.shape[1] // 2
    product = t_dot(left_ref[...], right_ref[...])
    half = product.shape[1] // 2
    lower = place_ref[0] == 0
    mine = jnp.where(lower, product[:, :width], product[:, half : half + width])
    other = jnp.where(lower, product[:, half : half + width], product[:, :width])
    first_ref[...] = mine
    first_sent_ref[...] = other.astype(bf16)
    last = jnp.concatenate([product[:, width:half], product[:, half + width :]], axis=1)
    near = place_ref[1] == 0
    last_ref[...] = jnp.where(near, last[:rows], last[rows:])
    last_sent_ref[...] = jnp.where(near, last[rows:], last[:rows]).astype(bf16)


def scatter_sends(left, right):
    if lax.axis_size("y") != 2:
        return None
    x_step = fsdp_bits()[-1]
    tokens, whole_rows = left.shape
    columns = right.shape[1]
    rows = whole_rows // lax.axis_size(FSDP)
    width = split_width(columns // 2)[0]
    place = jnp.stack([lax.axis_index("y"), bit_index(*x_step[:2])]).astype(jnp.int32)

    def out(count, wide, kind):
        return pl.BlockSpec((count, wide), lambda i, *_: (i, 0)), jax.ShapeDtypeStruct(
            (whole_rows // (2 * rows) * count, wide), kind
        )

    rest = columns - 2 * width
    outs = [out(2 * rows, width, bf16), out(2 * rows, width, f32), out(rows, rest, bf16), out(rows, rest, f32)]
    first_sent, first, last_sent, last = pl.pallas_call(
        functools.partial(product_kernel, width),
        grid_spec=pltpu.PrefetchScalarGridSpec(
            num_scalar_prefetch=1,
            grid=(whole_rows // (2 * rows),),
            in_specs=[
                pl.BlockSpec((tokens, 2 * rows), lambda i, *_: (0, i)),
                pl.BlockSpec((tokens, columns), lambda i, *_: (0, 0)),
            ],
            out_specs=[spec for spec, _ in outs],
        ),
        out_shape=[shape for _, shape in outs],
        compiler_params=pltpu.CompilerParams(vmem_limit_bytes=VMEM_LIMIT),
        cost_estimate=pl.CostEstimate(flops=0, bytes_accessed=0, transcendentals=0),
    )(place, left, right)
    return first, swap(first_sent, "y"), last, swap(last_sent, *x_step[:2])


def scatter_products(pairs, sends, rounds):
    steps = fsdp_bits()
    size = lax.axis_size(FSDP)
    if lax.axis_size("y") != 2:
        blocks = [t_dot(left, right) for left, right in pairs]
        blocks = [block.reshape((2,) * len(steps) + (block.shape[0] // size, -1)) for block in blocks]
        for number, step in enumerate(reversed(steps)):
            blocks = [scatter_step(block, step) for block in blocks]
            if number < 2:
                blocks = rounds[number](blocks)
        blocks = rounds[2](blocks)
        blocks = [block.astype(bf16).reshape(block.shape[-2:]) for block in blocks]
        return [sum_over(block, ("y",)).astype(bf16) for block in blocks]
    lane = len(steps) + 1
    y_step, x_step = ("y", 1, lane), steps[-1]
    y_index, x_index = lax.axis_index("y"), bit_index(*x_step[:2])
    firsts, lasts = [], []
    for first, first_sent, last, last_sent in sends:
        rows = first.shape[0] // size
        first = first + first_sent.astype(f32)
        last = last + last_sent.astype(f32)
        firsts.append(first.reshape((2,) * len(steps) + (rows, -1)))
        lasts.append(last.reshape((2,) * (len(steps) - 1) + (1, rows, 2, last.shape[1] // 2)))
    widths = [block.shape[-1] for block in firsts + lasts]
    first = jnp.concatenate(firsts, axis=lane)
    last = jnp.concatenate(lasts, axis=lane + 1)
    last = last.reshape(last.shape[:lane] + (-1,))
    first, last = rounds[0]((first, last))
    first, last = scatter_step(first, x_step), scatter_step(last, y_step)
    block = rounds[1](jnp.concatenate([first, last], axis=lane))
    for step in reversed(steps[:-1]):
        block = scatter_step(block, step)
    block = rounds[2](block).astype(bf16).reshape(block.shape[-2:])
    cuts = [sum(widths[: number + 1]) for number in range(len(widths) - 1)]
    halves = [jnp.split(half, cuts, axis=1) for half in jnp.split(order_by(y_index, block, swap(block, "y"), 1), 2, axis=1)]
    count = len(pairs)
    return [
        jnp.concatenate([half[number + part] for half in halves for part in (0, count)], axis=1)
        for number in range(count)
    ]


def head_probs(query, key):
    seq_len = query.shape[0]
    scores = dot_t(query, key) * HEAD_DIM ** (-0.5)
    rows = lax.broadcasted_iota(jnp.int32, (seq_len, seq_len), 0)
    columns = lax.broadcasted_iota(jnp.int32, (seq_len, seq_len), 1)
    scores = jnp.where(rows >= columns, scores, -1e30)
    exponent = jnp.exp(scores - jnp.max(scores, axis=-1, keepdims=True))
    return exponent / jnp.sum(exponent, axis=-1, keepdims=True)


def attend_kernel(xn_ref, weight_ref, joint_ref, attended_ref):
    joint = dot(xn_ref[...], weight_ref[...]).astype(bf16)
    joint_ref[...] = joint
    width = HEADS // 2 * HEAD_DIM
    key, value = joint[:, width : width + HEAD_DIM], joint[:, width + HEAD_DIM :]
    for head in range(HEADS // 2):
        columns = slice(head * HEAD_DIM, (head + 1) * HEAD_DIM)
        probs = head_probs(joint[:, columns], key).astype(bf16)
        attended_ref[:, columns] = dot(probs, value).astype(bf16)


def attend(xn_pair, weight, seq_len):
    rows, model_width = xn_pair.shape
    width = weight.shape[1]
    query_width = HEADS // 2 * HEAD_DIM
    return pl.pallas_call(
        attend_kernel,
        grid=(rows // seq_len,),
        in_specs=[
            pl.BlockSpec((seq_len, model_width), lambda i: (i, 0)),
            pl.BlockSpec((model_width, width), lambda i: (0, 0)),
        ],
        out_specs=[
            pl.BlockSpec((seq_len, width), lambda i: (i, 0)),
            pl.BlockSpec((seq_len, query_width), lambda i: (i, 0)),
        ],
        out_shape=[
            jax.ShapeDtypeStruct((rows, width), bf16),
            jax.ShapeDtypeStruct((rows, query_width), bf16),
        ],
        compiler_params=pltpu.CompilerParams(vmem_limit_bytes=VMEM_LIMIT),
        cost_estimate=pl.CostEstimate(flops=0, bytes_accessed=0, transcendentals=0),
    )(xn_pair, weight)


def attend_backward_kernel(joint_ref, grad_ref, weight_ref, grad_joint_ref, grad_xn_ref):
    scale = HEAD_DIM ** (-0.5)
    width = HEADS // 2 * HEAD_DIM
    joint = joint_ref[...]
    grad = grad_ref[...]
    key, value = joint[:, width : width + HEAD_DIM], joint[:, width + HEAD_DIM :]
    grad_key = jnp.zeros(key.shape, f32)
    grad_value = jnp.zeros(value.shape, f32)
    for head in range(HEADS // 2):
        columns = slice(head * HEAD_DIM, (head + 1) * HEAD_DIM)
        query, grad_head = joint[:, columns], grad[:, columns]
        probs = head_probs(query, key)
        grad_probs = dot_t(grad_head, value)
        delta = jnp.sum(probs * grad_probs, axis=-1, keepdims=True)
        grad_scores = (probs * (grad_probs - delta)).astype(bf16)
        grad_joint_ref[:, columns] = (dot(grad_scores, key) * scale).astype(bf16)
        grad_key = grad_key + t_dot(grad_scores, query)
        grad_value = grad_value + t_dot(probs.astype(bf16), grad_head)
    grad_joint_ref[:, width : width + HEAD_DIM] = (grad_key * scale).astype(bf16)
    grad_joint_ref[:, width + HEAD_DIM :] = grad_value.astype(bf16)
    grad_xn_ref[...] = dot_t(grad_joint_ref[...], weight_ref[...])


def attend_backward(joint, grad_attended, weight, seq_len):
    rows, width = joint.shape
    model_width = weight.shape[0]
    query_width = HEADS // 2 * HEAD_DIM
    return pl.pallas_call(
        attend_backward_kernel,
        grid=(rows // seq_len,),
        in_specs=[
            pl.BlockSpec((seq_len, width), lambda i: (i, 0)),
            pl.BlockSpec((seq_len, query_width), lambda i: (i, 0)),
            pl.BlockSpec((model_width, width), lambda i: (0, 0)),
        ],
        out_specs=[
            pl.BlockSpec((seq_len, width), lambda i: (i, 0)),
            pl.BlockSpec((seq_len, model_width), lambda i: (i, 0)),
        ],
        out_shape=[
            jax.ShapeDtypeStruct((rows, width), bf16),
            jax.ShapeDtypeStruct((rows, model_width), f32),
        ],
        compiler_params=pltpu.CompilerParams(vmem_limit_bytes=VMEM_LIMIT),
        cost_estimate=pl.CostEstimate(flops=0, bytes_accessed=0, transcendentals=0),
    )(joint, grad_attended, weight)


def expert_kernel(
    expert_ref,
    rows_ref,
    grad_ref,
    router_ref,
    up_ref,
    down_ref,
    inner_ref,
    out_ref,
    d_out_ref,
    d_projected_ref,
    d_in_ref,
):
    rows = rows_ref[...]
    width = rows.shape[1]
    mask = grad_ref[:, width : width + EXPERTS] > 0
    logits = jnp.where(mask, dot(rows, router_ref[...]), -1e30)
    exponent = jnp.where(mask, jnp.exp(logits - jnp.max(logits, axis=-1, keepdims=True)), 0.0)
    total = jnp.sum(exponent, axis=-1, keepdims=True)
    mine = lax.broadcasted_iota(jnp.int32, exponent.shape, 1) == expert_ref[0]
    gate = jnp.sum(jnp.where(mine, exponent, 0.0), axis=-1, keepdims=True)
    gate = gate / jnp.where(total > 0, total, 1.0)

    projected = dot(rows, up_ref[...])
    lower, upper = projected[:, :FFE], projected[:, FFE:]
    slope = (2.0 / 3.141592653589793) ** 0.5
    bend = jnp.tanh(slope * (lower + 0.044715 * lower * lower * lower))
    gelu = 0.5 * lower * (1.0 + bend)
    gelu_grad = 0.5 * (1.0 + bend) + 0.5 * lower * (1.0 - bend * bend) * slope * (
        1.0 + 3 * 0.044715 * lower * lower
    )
    inner = (gelu * upper).astype(bf16)
    inner_ref[...] = inner
    out = dot(inner, down_ref[...]).astype(bf16)
    out_ref[...] = out
    grad = grad_ref[:, :width].astype(f32)
    d_gate = jnp.sum(out.astype(f32) * grad, axis=-1, keepdims=True)
    d_gate_high = d_gate.astype(bf16).astype(f32)
    column = lax.broadcasted_iota(jnp.int32, (rows.shape[0], EXTRA), 1)
    d_in_ref[:, width:] = jnp.where(
        column == expert_ref[1],
        d_gate_high,
        jnp.where(column == expert_ref[1] + EXPERTS // 2, d_gate - d_gate_high, 0.0),
    ).astype(bf16)
    d_out = (gate * grad).astype(bf16)
    d_out_ref[...] = d_out
    d_inner = dot_t(d_out, down_ref[...])
    d_projected_ref[:, :FFE] = (d_inner * upper * gelu_grad).astype(bf16)
    d_projected_ref[:, FFE:] = (d_inner * gelu).astype(bf16)
    d_in_ref[:, :width] = dot_t(d_projected_ref[...], up_ref[...]).astype(bf16)


def expert_part(expert, received, grad_rows, router, up, down):
    rows, model_width = received.shape
    block = 256

    def row_block(width):
        return pl.BlockSpec((block, width), lambda i, *_: (i, 0))

    def whole(array):
        return pl.BlockSpec(array.shape, lambda i, *_: (0, 0))

    widths = (FFE, model_width, model_width, 2 * FFE, model_width + EXTRA)
    return pl.pallas_call(
        expert_kernel,
        grid_spec=pltpu.PrefetchScalarGridSpec(
            num_scalar_prefetch=1,
            grid=(rows // block,),
            in_specs=[
                row_block(model_width),
                row_block(model_width + EXTRA),
                whole(router),
                whole(up),
                whole(down),
            ],
            out_specs=[row_block(width) for width in widths],
        ),
        out_shape=[jax.ShapeDtypeStruct((rows, width), bf16) for width in widths],
        compiler_params=pltpu.CompilerParams(vmem_limit_bytes=VMEM_LIMIT),
        cost_estimate=pl.CostEstimate(flops=0, bytes_accessed=0, transcendentals=0),
    )(expert, received, grad_rows, router, up, down)


def token_backward_kernel(
    core_ref,
    place_ref,
    back_ref,
    far_ref,
    spread_ref,
    gates_ref,
    router_ref,
    xn_ref,
    hidden_ref,
    gain_ref,
    grad_ref,
    weight_ref,
    d_hidden_ref,
    d_hidden_b_ref,
    d_attended_ref,
    small_ref,
):
    width = hidden_ref.shape[1]
    part = EXPERTS // 2
    wide = t_dot(place_ref[...], back_ref[...])
    far = far_ref[...]
    d_gates = jnp.zeros(gates_ref.shape, f32)
    for number, extra in enumerate((wide[:, width:].astype(bf16), far[:, width:])):
        for start in (0, part):
            d_gates = d_gates + dot(extra[:, start : start + part], spread_ref[number])
    gates = gates_ref[...]
    d_chosen = gates * (d_gates - jnp.sum(gates * d_gates, axis=-1, keepdims=True))
    d_logits = d_chosen.astype(bf16)
    d_xn = dot_t(d_logits, router_ref[...]) + wide[:, :width] + far[:, :width].astype(f32)
    hidden = hidden_ref[...]
    scale = lax.rsqrt(jnp.mean(hidden * hidden, axis=-1, keepdims=True) + EPSILON)
    normed = hidden * scale
    scaled = d_xn * gain_ref[...]
    d_hidden = grad_ref[...].astype(f32) + scale * (
        scaled - normed * jnp.mean(scaled * normed, axis=-1, keepdims=True)
    )
    d_hidden_ref[...] = d_hidden
    d_hidden_b = d_hidden.astype(bf16)
    d_hidden_b_ref[...] = d_hidden_b
    small_ref[:EXPERTS] = t_dot(d_logits, xn_ref[...])
    small_ref[EXPERTS:] = jnp.broadcast_to(jnp.sum(d_xn * normed, axis=0, keepdims=True), (8, width))
    d_attended = dot_t(d_hidden_b, weight_ref[...]).astype(bf16)
    first, last = d_attended[:, : width // 2], d_attended[:, width // 2 :]
    lower = core_ref[0] == 0
    d_attended_ref[0] = jnp.where(lower, first, last)
    d_attended_ref[1] = jnp.where(lower, last, first)


def token_backward(core, place, back, far, spread, gates, router, xn, hidden, gain, grad, weight):
    seq_len, width = hidden.shape
    return pl.pallas_call(
        token_backward_kernel,
        in_specs=[pl.BlockSpec(memory_space=pltpu.SMEM)] + [pl.BlockSpec(memory_space=pltpu.VMEM)] * 11,
        out_specs=[pl.BlockSpec(memory_space=pltpu.VMEM)] * 4,
        out_shape=[
            jax.ShapeDtypeStruct((seq_len, width), f32),
            jax.ShapeDtypeStruct((seq_len, width), bf16),
            jax.ShapeDtypeStruct((2, seq_len, width // 2), bf16),
            jax.ShapeDtypeStruct((EXPERTS + 8, width), f32),
        ],
        compiler_params=pltpu.CompilerParams(vmem_limit_bytes=VMEM_LIMIT),
        cost_estimate=pl.CostEstimate(flops=0, bytes_accessed=0, transcendentals=0),
    )(core, place, back, far, spread, gates, router, xn, hidden, gain, grad, weight)


def expert_weights_kernel(x_own, x_far, p_own, p_far, i_own, i_far, d_own, d_far, up_ref, down_ref):
    up_ref[...] = (t_dot(x_own[...], p_own[...]) + t_dot(x_far[...], p_far[...])).astype(bf16)
    down_ref[...] = (t_dot(i_own[...], d_own[...]) + t_dot(i_far[...], d_far[...])).astype(bf16)


def expert_weights(received, d_projected, inner, d_out):
    rows, model_width = received[0].shape
    steps = 3

    def columns(array):
        return pl.BlockSpec((rows, array.shape[1] // steps), lambda i: (0, i))

    def whole(array):
        return pl.BlockSpec(array.shape, lambda i: (0, 0))

    return pl.pallas_call(
        expert_weights_kernel,
        grid=(steps,),
        in_specs=[columns(a) for a in received]
        + [whole(a) for a in d_projected]
        + [columns(a) for a in inner]
        + [whole(a) for a in d_out],
        out_specs=[
            pl.BlockSpec((model_width // steps, 2 * FFE), lambda i: (i, 0)),
            pl.BlockSpec((FFE // steps, model_width), lambda i: (i, 0)),
        ],
        out_shape=[
            jax.ShapeDtypeStruct((model_width, 2 * FFE), bf16),
            jax.ShapeDtypeStruct((FFE, model_width), bf16),
        ],
        compiler_params=pltpu.CompilerParams(vmem_limit_bytes=VMEM_LIMIT),
        cost_estimate=pl.CostEstimate(flops=0, bytes_accessed=0, transcendentals=0),
    )(*received, *d_projected, *inner, *d_out)


def shards(
    tokens,
    routes,
    norm_attn,
    qkv_weight,
    out_weight,
    norm_moe,
    router_weight,
    gate_up,
    down,
    grad_output,
):
    seq_len, model_width = tokens.shape
    query_half = HEADS * HEAD_DIM // 2
    kv_half = KV_HEADS * HEAD_DIM // 2
    out_half = out_weight.shape[1] // 2
    groups = lax.axis_size(EXPERT)
    fsdp = lax.axis_size(FSDP)
    half_devices = groups * fsdp // 2
    local_count = gate_up.shape[0]
    parts = fsdp // local_count
    half_experts = EXPERTS // 2
    rows = half_experts * CAP
    core = lax.axis_index("c")
    half = lax.axis_index("h")
    me = lax.axis_index(FSDP)
    group = lax.axis_index(EXPERT)
    my_expert = jnp.stack(
        [
            group * local_count + me // parts,
            group * (local_count // 2) + me // parts - half * (local_count // 2),
        ]
    ).astype(jnp.int32)

    box = {}

    def tie(value, *names):
        value, held = together(value, [box[name] for name in names])
        box.update(zip(names, held))
        return value

    up_width, down_width = gate_up.shape[1], down.shape[1]
    columns = fsdp // 4

    def target(index, move, sign=1):
        step, cross = move
        line = index // columns
        line = (line + sign * step + 4) % 4 if step >= 0 else line ^ -step
        return line * columns + (index % columns ^ cross)

    def every(moves):
        return [
            (step, other) for step, cross in moves for other in (range(1, columns) if cross else range(1))
        ]

    def fetch(moves, *names):
        for move in every(moves):
            expert = target(me, move) // parts
            piece = jnp.concatenate(
                [
                    lax.dynamic_index_in_dim(gate_up, expert, 0, keepdims=False),
                    lax.dynamic_index_in_dim(down, expert, 0, keepdims=False),
                ],
                axis=0,
            )
            if move != (0, 0):
                piece = lax.ppermute(tie(piece, *names), FSDP, [(i, target(i, move)) for i in range(fsdp)])
            box["in", move] = piece

    def coming(moves):
        return [("in", move) for move in every(moves)]

    def assemble():
        up_full = jnp.zeros((fsdp * up_width, gate_up.shape[2]), gate_up.dtype)
        down_full = jnp.zeros((fsdp * down_width, down.shape[2]), down.dtype)
        for move in every(sum(INWARD, [(0, 0)])):
            source, piece = target(me, move, -1), box["in", move]
            up_full = lax.dynamic_update_slice(up_full, piece[:up_width], (source * up_width, 0))
            down_full = lax.dynamic_update_slice(down_full, piece[up_width:], (source * down_width, 0))
        return up_full, down_full

    def give(moves, up_grad, down_grad, *names):
        for move in every(moves):
            to = target(me, move)
            piece = jnp.concatenate(
                [
                    lax.dynamic_slice_in_dim(up_grad, to * up_width, up_width, axis=0),
                    lax.dynamic_slice_in_dim(down_grad, to * down_width, down_width, axis=0),
                ],
                axis=0,
            )
            if move != (0, 0):
                piece = lax.ppermute(tie(piece, *names), FSDP, [(i, target(i, move)) for i in range(fsdp)])
            box["out", move] = piece

    def going(moves):
        return [("out", move) for move in every(moves)]

    def collect():
        up_sum = jnp.zeros(gate_up.shape, f32)
        down_sum = jnp.zeros(down.shape, f32)
        for move in every(sum(OUTWARD, [(0, 0)])):
            expert = target(me, move, -1) // parts
            piece = box["out", move].astype(f32)[None]
            up_part, down_part = piece[:, :up_width], piece[:, up_width:]
            if parts > 1:
                up_part = up_part + lax.dynamic_slice_in_dim(up_sum, expert, 1, axis=0)
                down_part = down_part + lax.dynamic_slice_in_dim(down_sum, expert, 1, axis=0)
            up_sum = lax.dynamic_update_slice(up_sum, up_part, (expert, 0, 0))
            down_sum = lax.dynamic_update_slice(down_sum, down_part, (expert, 0, 0))
        return up_sum, down_sum

    def exchange(buffer):
        shape = buffer.shape
        return lax.all_to_all(
            buffer.reshape((half_devices, rows // half_devices) + shape[1:]),
            HALF,
            split_axis=0,
            concat_axis=0,
            tiled=True,
        ).reshape(shape)

    def half_columns(table, index):
        cube = table.reshape(table.shape[0], groups, 2, local_count // 2)
        return lax.dynamic_index_in_dim(cube, index, 2, keepdims=False).reshape(table.shape[0], half_experts)

    token_f = tokens.astype(f32)

    qkv_mine = jnp.concatenate(
        [
            lax.dynamic_slice_in_dim(qkv_weight, core * query_half, query_half, axis=1),
            lax.dynamic_slice_in_dim(qkv_weight, 2 * query_half + core * kv_half, kv_half, axis=1),
            lax.dynamic_slice_in_dim(qkv_weight, 2 * query_half + (2 + core) * kv_half, kv_half, axis=1),
        ],
        axis=1,
    )
    out_mine = lax.dynamic_slice_in_dim(out_weight, core * out_half, out_half, axis=1)
    expert_ids = jnp.arange(EXPERTS, dtype=jnp.int32)
    order = jnp.arange(seq_len)
    earlier = (order[None, :] < order[:, None]).astype(bf16)

    def placing(routing):
        mask = jnp.any(routing[:, :, None] == expert_ids[None, None, :], axis=1)
        position = dot(earlier, mask.astype(bf16)).astype(jnp.int32)
        slot = half_columns(jnp.where(mask, position, -1), half).T
        place = slot[:, None, :] == jnp.arange(CAP, dtype=jnp.int32)[None, :, None]
        return mask, place

    mask_own, cube_own = placing(routes)
    mask_far, cube_far = placing(swap(routes, "h"))
    place_own = cube_own.astype(bf16).reshape(rows, seq_len)
    place_far = cube_far.astype(bf16).reshape(rows, seq_len)

    def first_done(block):
        nonlocal gate_up, down
        sent, block, gate_up, down = together(grad_output, block, gate_up, down)
        box["grad_far"] = swap(sent, "h")
        fetch(INWARD[0])
        return mark(block)

    def send_rows(place, grad, mask):
        extra = jnp.pad(mask.astype(bf16), ((0, 0), (0, EXTRA - EXPERTS)))
        return dot(place, jnp.concatenate([grad, extra], axis=1)).astype(bf16)

    xn_first_f, norm_first_pull = jax.vjp(rms_apply, token_f, norm_attn)
    xn_first = xn_first_f.astype(bf16)
    xn_pair = jnp.concatenate([xn_first, swap(xn_first, "c")], axis=0)
    shard = jnp.concatenate([qkv_mine, out_mine], axis=1)
    core_weights, xn_pair, own_sent = tie(
        (gather_shards(shard, first_done), xn_pair, send_rows(place_own, grad_output, mask_own)),
        "grad_far",
        *coming(INWARD[0]),
    )
    fetch(INWARD[1], *coming(INWARD[0]))
    box["grad_rows_own"] = exchange(own_sent)
    xn_pair = mark(xn_pair)
    qkv_width = query_half + 2 * kv_half
    qkv_core, out_core = core_weights[:, :qkv_width], core_weights[:, qkv_width:]

    joint, attended_mine = attend(xn_pair, qkv_core, seq_len)
    out_full = order_by(core, out_core, swap(out_core, "c"), 1)
    attended_mine = attended_mine.reshape(2, seq_len, query_half)
    far_sent = send_rows(place_far, box["grad_far"], mask_far)
    attended_mine, far_sent = tie((attended_mine, far_sent), "grad_rows_own", *coming(INWARD[1]))
    fetch(INWARD[2], *coming(INWARD[1]))
    box["grad_rows_far"] = exchange(far_sent)
    attended_mine = mark(attended_mine)
    attended_other = swap(attended_mine, "c")
    attended = order_by(core, attended_mine[0], attended_other[1], 1)
    attended_next = order_by(core, attended_mine[1], attended_other[0], 1)
    hidden = token_f + dot(attended, out_full)
    xn_second = rms_apply(hidden, norm_moe).astype(bf16)

    def gating(values_b, mask):
        logits = dot(values_b, router_weight)
        top = jnp.max(jnp.where(mask, logits, -1e30), axis=-1, keepdims=True)
        exponent = jnp.where(mask, jnp.exp(jnp.where(mask, logits - top, 0.0)), 0.0)
        total = jnp.sum(exponent, axis=-1, keepdims=True)
        return exponent / jnp.where(total > 0, total, 1.0)

    own_sent, xn_sent = tie(
        (dot(place_own, xn_second).astype(bf16), xn_second), "grad_rows_far", *coming(INWARD[2])
    )
    fetch(INWARD[3], *coming(INWARD[2]))
    box["received_own"] = exchange(mark(own_sent))
    fetch([(0, 0)])
    box["in", (0, 0)] = mark(tie(box["in", (0, 0)], *coming(INWARD[2])))
    xn_sent = tie(xn_sent, "received_own", *coming(INWARD[3]))
    box["xn_far"] = swap(xn_sent, "h")
    fetch(INWARD[4], *coming(INWARD[3]))
    far_sent = tie(dot(place_far, box["xn_far"]).astype(bf16), *coming(INWARD[4]))
    box["received_far"] = exchange(far_sent)
    gate_up_full, down_full = assemble()
    box["own"] = expert_part(
        my_expert, box["received_own"], box["grad_rows_own"], router_weight, gate_up_full, down_full
    )
    xn_far = box["xn_far"]
    gates = gating(xn_second, mask_own)
    gates_far = gating(xn_far, mask_far)

    box["back_in_own"] = exchange(tie(box["own"][4], "received_far"))
    box["far"] = expert_part(
        my_expert, box["received_far"], box["grad_rows_far"], router_weight, gate_up_full, down_full
    )
    received, d_projected, inner, d_out = [
        list(pair)
        for pair in zip(
            (box["received_own"], box["own"][3], box["own"][0], box["own"][2]),
            (box["received_far"], box["far"][3], box["far"][0], box["far"][2]),
        )
    ]
    up_grad, down_grad = expert_weights(received, d_projected, inner, d_out)
    sent, up_grad, down_grad = tie((box["far"][4], up_grad, down_grad), "back_in_own")
    box["back_in_far"] = exchange(sent)
    give(OUTWARD[0], up_grad, down_grad)
    box["d_in_sum_far"] = swap(t_dot(place_far, box["back_in_far"]).astype(bf16), "h")
    give([(0, 0)], up_grad, down_grad)

    places = jnp.arange(EXPERTS) // local_count * (local_count // 2) + jnp.arange(EXPERTS) % (local_count // 2)
    side = jnp.arange(EXPERTS) % local_count // (local_count // 2)
    mine = (places[None, :] == jnp.arange(half_experts)[:, None]).astype(bf16)
    spread = jnp.stack([mine * (side == half), mine * (side != half)]).astype(bf16)
    d_hidden, d_hidden_b, d_attended, router_moe = token_backward(
        core.reshape(1).astype(jnp.int32),
        place_own,
        box["back_in_own"],
        box["d_in_sum_far"],
        spread,
        gates,
        router_weight,
        xn_second,
        hidden,
        norm_moe[None],
        grad_output,
        out_full,
    )

    def mix(cube, gate, back):
        spread = jnp.where(cube, half_columns(gate, half).T[:, None, :], 0.0).reshape(rows, seq_len)
        high = spread.astype(bf16)
        low = (spread - high.astype(f32)).astype(bf16)
        return t_dot(high, back) + t_dot(low, back)

    d_hidden_b, up_grad, down_grad, out_far = together(d_hidden_b, up_grad, down_grad, box["far"][1])
    give(OUTWARD[1], up_grad, down_grad)
    box["back_out_far"] = exchange(mark(out_far))

    def halves(value):
        first, last = jnp.split(value, 2, axis=1)
        return jnp.where(core == 0, first, last), jnp.where(core == 0, last, first)

    grad_heads = jnp.stack([d_attended[0], swap(d_attended[1], "c")]).reshape(2 * seq_len, query_half)
    d_hid_mine, d_hid_send = halves(d_hidden_b)
    d_hid_next = swap(d_hid_send, "c")
    out_pair = (
        jnp.concatenate([attended, attended_next], axis=0),
        jnp.concatenate([d_hid_mine, d_hid_next], axis=0),
    )
    out_sends = scatter_sends(*out_pair)
    grad_heads = mark(grad_heads)
    grad_joint, d_xn_pair = attend_backward(joint, grad_heads, qkv_core, seq_len)
    grad_joint, out_own = tie((grad_joint, box["own"][1]), "back_out_far")
    box["back_out_own"] = exchange(out_own)
    moe_sent = mix(cube_far, gates_far, box["back_out_far"]).astype(bf16)

    def first_round(blocks):
        blocks, sent, box["small"] = tie((blocks, moe_sent, box["small"]), *going(OUTWARD[0] + OUTWARD[1]))
        give(OUTWARD[2], up_grad, down_grad)
        box["moe_far"] = swap(sent, "h")
        box["small"] = sum_over(box["small"], ("c", "y", "r", "h"))
        return blocks

    def second_round(blocks):
        blocks = tie(blocks, "moe_far", *going(OUTWARD[2]))
        give(OUTWARD[3], up_grad, down_grad, *going(OUTWARD[2]))
        return blocks

    def third_round(blocks):
        return tie(blocks, *going(OUTWARD[3]))

    d_xn_first = d_xn_pair[:seq_len] + swap(d_xn_pair[seq_len:], "c")
    d_token_norm, gain_attn_local = norm_first_pull(d_xn_first)
    grad_tokens = d_hidden + d_token_norm

    box["small"] = jnp.concatenate([router_moe[: EXPERTS + 1], gain_attn_local[None]], axis=0)
    qkv_grad, out_grad = scatter_products(
        ((xn_pair, grad_joint), out_pair),
        (scatter_sends(xn_pair, grad_joint), out_sends),
        (first_round, second_round, third_round),
    )
    moe_own = mix(cube_own, gates, box["back_out_own"])
    small = box["small"]
    mixed = (hidden + (moe_own + box["moe_far"].astype(f32))).astype(bf16)
    grad_gate_up, grad_down = collect()
    grad_out_proj = order_by(core, out_grad.astype(f32), swap(out_grad, "c").astype(f32), 1)
    qkv_grad_other = swap(qkv_grad, "c")
    first = jnp.where(core == 0, qkv_grad, qkv_grad_other).astype(f32)
    last = jnp.where(core == 0, qkv_grad_other, qkv_grad).astype(f32)
    cut = (query_half, query_half + kv_half)
    grad_qkv = jnp.concatenate(
        [piece for pair in zip(jnp.split(first, cut, axis=1), jnp.split(last, cut, axis=1)) for piece in pair],
        axis=1,
    )

    return (
        mixed,
        grad_tokens,
        small[EXPERTS + 1],
        grad_qkv,
        grad_out_proj,
        small[EXPERTS],
        small[:EXPERTS].T,
        grad_gate_up,
        grad_down,
    )


def solution(mesh):
    expert, fsdp = mesh.devices.shape
    fine = Mesh(mesh.devices.reshape(expert // 2, 2, 2, fsdp // 2), BOTH)
    in_specs = (
        P(BOTH, None),
        P(BOTH, None),
        P(),
        P(FSDP, None),
        P(FSDP, None),
        P(),
        P(),
        P(EXPERT, FSDP, None),
        P(EXPERT, FSDP, None),
        P(BOTH, None),
    )
    out_specs = (
        P(BOTH, None),
        P(BOTH, None),
        P(),
        P(FSDP, None),
        P(FSDP, None),
        P(),
        P(),
        P(EXPERT, FSDP, None),
        P(EXPERT, FSDP, None),
    )
    return jax.shard_map(shards, mesh=fine, in_specs=in_specs, out_specs=out_specs, check_vma=False)
```

```python
import functools

import jax
import jax.numpy as jnp
from jax import lax
from jax.experimental import pallas as pl
from jax.experimental.pallas import tpu as pltpu
from jax.sharding import Mesh
from jax.sharding import PartitionSpec as P

HEADS = 12
KV_HEADS = 2
HEAD_DIM = 128
FFE = 768
EXPERTS = 32
CAP = 48
EPSILON = 1e-06
VMEM_LIMIT = 56 * 1024 * 1024
EXTRA = 128
INWARD = [[(-1, 0), (-2, 0), (0, 1)], [(-3, 0)], [(-2, 1)], [(-3, 1)], [(-1, 1)]]
OUTWARD = [[(1, 0)], [(3, 0), (2, 0)], [(2, 1)], [(1, 1), (3, 1), (0, 1)]]
EXPERT = ("y", "c")
FSDP = ("h", "r")
BOTH = EXPERT + FSDP
HALF = ("y", "c", "r")
f32 = jnp.float32
bf16 = jnp.bfloat16


def dot(a, b):
    return jnp.dot(a, b, preferred_element_type=f32)


def dot_t(a, b):
    return lax.dot_general(a, b, (((1,), (1,)), ((), ())), preferred_element_type=f32)


def t_dot(a, b):
    return lax.dot_general(a, b, (((0,), (0,)), ((), ())), preferred_element_type=f32)


def rms_apply(values, gain):
    return values * lax.rsqrt(jnp.mean(values * values, axis=-1, keepdims=True) + EPSILON) * gain


def swap(value, axis, bit=1):
    size = lax.axis_size(axis)
    return lax.ppermute(value, axis, [(i, i ^ bit) for i in range(size)])


def sum_over(value, axes):
    for axis in axes:
        bit = 1
        while bit < lax.axis_size(axis):
            value = value + swap(value, axis, bit)
            bit *= 2
    return value


def together(*values):
    return lax.optimization_barrier(values)


def marker_kernel(*refs):
    pass


def mark(values):
    flat, tree = jax.tree.flatten(values)
    anywhere = [pl.BlockSpec(memory_space=pl.ANY)] * len(flat)
    same = pl.pallas_call(
        marker_kernel,
        in_specs=anywhere,
        out_specs=anywhere,
        out_shape=[jax.ShapeDtypeStruct(value.shape, value.dtype) for value in flat],
        input_output_aliases={number: number for number in range(len(flat))},
        cost_estimate=pl.CostEstimate(flops=10**12, bytes_accessed=0, transcendentals=0),
    )(*flat)
    return jax.tree.unflatten(tree, same)


def order_by(index, mine, other, axis):
    size = mine.shape[axis]
    shape = mine.shape[:axis] + (2 * size,) + mine.shape[axis + 1 :]
    start = [0] * mine.ndim
    start[axis] = index * size
    both = lax.dynamic_update_slice(jnp.zeros(shape, mine.dtype), mine, start)
    start[axis] = (1 - index) * size
    return lax.dynamic_update_slice(both, other, start)


def part_of(value, index, axis):
    size = value.shape[axis] // 2
    return lax.dynamic_slice_in_dim(value, index * size, size, axis=axis)


def split_width(width):
    first = (width // 2 + 127) // 128 * 128
    return first, width - first


def fsdp_bits():
    size = lax.axis_size("r")
    bits = [("h", 1, 0)]
    bit = size // 2
    while bit:
        bits.append(("r", bit, len(bits)))
        bit //= 2
    return bits


def bit_index(axis, bit):
    return (lax.axis_index(axis) // bit) % 2


def gather_step(block, step):
    axis, bit, dim = step
    return order_by(bit_index(axis, bit), block, swap(block, axis, bit), dim)


def scatter_step(block, step):
    axis, bit, dim = step
    index = bit_index(axis, bit)
    other = swap(part_of(block, 1 - index, dim).astype(bf16), axis, bit)
    return part_of(block, index, dim).astype(f32) + other.astype(f32)


def gather_shards(shard, first_done):
    steps = fsdp_bits()
    rows, columns = shard.shape
    whole_rows = rows * lax.axis_size(FSDP)
    shape = (1,) * len(steps) + (rows, columns)
    if lax.axis_size("y") != 2:
        block = shard.reshape(shape)
        for step in steps:
            block = gather_step(block, step)
        return first_done(block).reshape(whole_rows, columns)
    lane = len(steps) + 1
    y_step, x_step = ("y", 1, lane), steps[-1]
    block = part_of(shard.reshape(shape), lax.axis_index("y"), lane)
    for step in steps[:-1]:
        block = gather_step(block, step)
    block = first_done(block)
    first, last = jnp.split(block, [split_width(columns // 2)[0]], axis=lane)
    first, last = gather_step(first, x_step), gather_step(last, y_step)
    first, last = gather_step(first, y_step), gather_step(last, x_step)
    parts = [
        piece for pair in zip(jnp.split(first, 2, axis=lane), jnp.split(last, 2, axis=lane)) for piece in pair
    ]
    return jnp.concatenate(parts, axis=lane).reshape(whole_rows, columns)


def product_kernel(width, place_ref, left_ref, right_ref, first_sent_ref, first_ref, last_sent_ref, last_ref):
    rows = left_ref.shape[1] // 2
    product = t_dot(left_ref[...], right_ref[...])
    half = product.shape[1] // 2
    lower = place_ref[0] == 0
    mine = jnp.where(lower, product[:, :width], product[:, half : half + width])
    other = jnp.where(lower, product[:, half : half + width], product[:, :width])
    first_ref[...] = mine
    first_sent_ref[...] = other.astype(bf16)
    last = jnp.concatenate([product[:, width:half], product[:, half + width :]], axis=1)
    near = place_ref[1] == 0
    last_ref[...] = jnp.where(near, last[:rows], last[rows:])
    last_sent_ref[...] = jnp.where(near, last[rows:], last[:rows]).astype(bf16)


def scatter_sends(left, right):
    if lax.axis_size("y") != 2:
        return None
    x_step = fsdp_bits()[-1]
    tokens, whole_rows = left.shape
    columns = right.shape[1]
    rows = whole_rows // lax.axis_size(FSDP)
    width = split_width(columns // 2)[0]
    place = jnp.stack([lax.axis_index("y"), bit_index(*x_step[:2])]).astype(jnp.int32)

    def out(count, wide, kind):
        return pl.BlockSpec((count, wide), lambda i, *_: (i, 0)), jax.ShapeDtypeStruct(
            (whole_rows // (2 * rows) * count, wide), kind
        )

    rest = columns - 2 * width
    outs = [out(2 * rows, width, bf16), out(2 * rows, width, f32), out(rows, rest, bf16), out(rows, rest, f32)]
    first_sent, first, last_sent, last = pl.pallas_call(
        functools.partial(product_kernel, width),
        grid_spec=pltpu.PrefetchScalarGridSpec(
            num_scalar_prefetch=1,
            grid=(whole_rows // (2 * rows),),
            in_specs=[
                pl.BlockSpec((tokens, 2 * rows), lambda i, *_: (0, i)),
                pl.BlockSpec((tokens, columns), lambda i, *_: (0, 0)),
            ],
            out_specs=[spec for spec, _ in outs],
        ),
        out_shape=[shape for _, shape in outs],
        compiler_params=pltpu.CompilerParams(vmem_limit_bytes=VMEM_LIMIT),
        cost_estimate=pl.CostEstimate(flops=0, bytes_accessed=0, transcendentals=0),
    )(place, left, right)
    return first, swap(first_sent, "y"), last, swap(last_sent, *x_step[:2])


def scatter_products(pairs, sends, rounds):
    steps = fsdp_bits()
    size = lax.axis_size(FSDP)
    if lax.axis_size("y") != 2:
        blocks = [t_dot(left, right) for left, right in pairs]
        blocks = [block.reshape((2,) * len(steps) + (block.shape[0] // size, -1)) for block in blocks]
        for number, step in enumerate(reversed(steps)):
            blocks = [scatter_step(block, step) for block in blocks]
            if number < 2:
                blocks = rounds[number](blocks)
        blocks = rounds[2](blocks)
        blocks = [block.astype(bf16).reshape(block.shape[-2:]) for block in blocks]
        return [sum_over(block, ("y",)).astype(bf16) for block in blocks]
    lane = len(steps) + 1
    y_step, x_step = ("y", 1, lane), steps[-1]
    y_index, x_index = lax.axis_index("y"), bit_index(*x_step[:2])
    firsts, lasts = [], []
    for first, first_sent, last, last_sent in sends:
        rows = first.shape[0] // size
        first = first + first_sent.astype(f32)
        last = last + last_sent.astype(f32)
        firsts.append(first.reshape((2,) * len(steps) + (rows, -1)))
        lasts.append(last.reshape((2,) * (len(steps) - 1) + (1, rows, 2, last.shape[1] // 2)))
    widths = [block.shape[-1] for block in firsts + lasts]
    first = jnp.concatenate(firsts, axis=lane)
    last = jnp.concatenate(lasts, axis=lane + 1)
    last = last.reshape(last.shape[:lane] + (-1,))
    first, last = rounds[0]((first, last))
    first, last = scatter_step(first, x_step), scatter_step(last, y_step)
    block = rounds[1](jnp.concatenate([first, last], axis=lane))
    for step in reversed(steps[:-1]):
        block = scatter_step(block, step)
    block = rounds[2](block).astype(bf16).reshape(block.shape[-2:])
    cuts = [sum(widths[: number + 1]) for number in range(len(widths) - 1)]
    halves = [jnp.split(half, cuts, axis=1) for half in jnp.split(order_by(y_index, block, swap(block, "y"), 1), 2, axis=1)]
    count = len(pairs)
    return [
        jnp.concatenate([half[number + part] for half in halves for part in (0, count)], axis=1)
        for number in range(count)
    ]


def head_probs(query, key):
    seq_len = query.shape[0]
    scores = dot_t(query, key) * HEAD_DIM ** (-0.5)
    rows = lax.broadcasted_iota(jnp.int32, (seq_len, seq_len), 0)
    columns = lax.broadcasted_iota(jnp.int32, (seq_len, seq_len), 1)
    scores = jnp.where(rows >= columns, scores, -1e30)
    exponent = jnp.exp(scores - jnp.max(scores, axis=-1, keepdims=True))
    return exponent / jnp.sum(exponent, axis=-1, keepdims=True)


def attend_kernel(xn_ref, weight_ref, joint_ref, attended_ref):
    joint = dot(xn_ref[...], weight_ref[...]).astype(bf16)
    joint_ref[...] = joint
    width = HEADS // 2 * HEAD_DIM
    key, value = joint[:, width : width + HEAD_DIM], joint[:, width + HEAD_DIM :]
    for head in range(HEADS // 2):
        columns = slice(head * HEAD_DIM, (head + 1) * HEAD_DIM)
        probs = head_probs(joint[:, columns], key).astype(bf16)
        attended_ref[:, columns] = dot(probs, value).astype(bf16)


def attend(xn_pair, weight, seq_len):
    rows, model_width = xn_pair.shape
    width = weight.shape[1]
    query_width = HEADS // 2 * HEAD_DIM
    return pl.pallas_call(
        attend_kernel,
        grid=(rows // seq_len,),
        in_specs=[
            pl.BlockSpec((seq_len, model_width), lambda i: (i, 0)),
            pl.BlockSpec((model_width, width), lambda i: (0, 0)),
        ],
        out_specs=[
            pl.BlockSpec((seq_len, width), lambda i: (i, 0)),
            pl.BlockSpec((seq_len, query_width), lambda i: (i, 0)),
        ],
        out_shape=[
            jax.ShapeDtypeStruct((rows, width), bf16),
            jax.ShapeDtypeStruct((rows, query_width), bf16),
        ],
        compiler_params=pltpu.CompilerParams(vmem_limit_bytes=VMEM_LIMIT),
        cost_estimate=pl.CostEstimate(flops=0, bytes_accessed=0, transcendentals=0),
    )(xn_pair, weight)


def attend_backward_kernel(joint_ref, grad_ref, weight_ref, grad_joint_ref, grad_xn_ref):
    scale = HEAD_DIM ** (-0.5)
    width = HEADS // 2 * HEAD_DIM
    joint = joint_ref[...]
    grad = grad_ref[...]
    key, value = joint[:, width : width + HEAD_DIM], joint[:, width + HEAD_DIM :]
    grad_key = jnp.zeros(key.shape, f32)
    grad_value = jnp.zeros(value.shape, f32)
    for head in range(HEADS // 2):
        columns = slice(head * HEAD_DIM, (head + 1) * HEAD_DIM)
        query, grad_head = joint[:, columns], grad[:, columns]
        probs = head_probs(query, key)
        grad_probs = dot_t(grad_head, value)
        delta = jnp.sum(probs * grad_probs, axis=-1, keepdims=True)
        grad_scores = (probs * (grad_probs - delta)).astype(bf16)
        grad_joint_ref[:, columns] = (dot(grad_scores, key) * scale).astype(bf16)
        grad_key = grad_key + t_dot(grad_scores, query)
        grad_value = grad_value + t_dot(probs.astype(bf16), grad_head)
    grad_joint_ref[:, width : width + HEAD_DIM] = (grad_key * scale).astype(bf16)
    grad_joint_ref[:, width + HEAD_DIM :] = grad_value.astype(bf16)
    grad_xn_ref[...] = dot_t(grad_joint_ref[...], weight_ref[...])


def attend_backward(joint, grad_attended, weight, seq_len):
    rows, width = joint.shape
    model_width = weight.shape[0]
    query_width = HEADS // 2 * HEAD_DIM
    return pl.pallas_call(
        attend_backward_kernel,
        grid=(rows // seq_len,),
        in_specs=[
            pl.BlockSpec((seq_len, width), lambda i: (i, 0)),
            pl.BlockSpec((seq_len, query_width), lambda i: (i, 0)),
            pl.BlockSpec((model_width, width), lambda i: (0, 0)),
        ],
        out_specs=[
            pl.BlockSpec((seq_len, width), lambda i: (i, 0)),
            pl.BlockSpec((seq_len, model_width), lambda i: (i, 0)),
        ],
        out_shape=[
            jax.ShapeDtypeStruct((rows, width), bf16),
            jax.ShapeDtypeStruct((rows, model_width), f32),
        ],
        compiler_params=pltpu.CompilerParams(vmem_limit_bytes=VMEM_LIMIT),
        cost_estimate=pl.CostEstimate(flops=0, bytes_accessed=0, transcendentals=0),
    )(joint, grad_attended, weight)


def expert_kernel(
    expert_ref,
    rows_ref,
    grad_ref,
    router_ref,
    up_ref,
    down_ref,
    inner_ref,
    out_ref,
    d_out_ref,
    d_projected_ref,
    d_in_ref,
):
    rows = rows_ref[...]
    width = rows.shape[1]
    mask = grad_ref[:, width : width + EXPERTS] > 0
    logits = jnp.where(mask, dot(rows, router_ref[...]), -1e30)
    exponent = jnp.where(mask, jnp.exp(logits - jnp.max(logits, axis=-1, keepdims=True)), 0.0)
    total = jnp.sum(exponent, axis=-1, keepdims=True)
    mine = lax.broadcasted_iota(jnp.int32, exponent.shape, 1) == expert_ref[0]
    gate = jnp.sum(jnp.where(mine, exponent, 0.0), axis=-1, keepdims=True)
    gate = gate / jnp.where(total > 0, total, 1.0)

    projected = dot(rows, up_ref[...])
    lower, upper = projected[:, :FFE], projected[:, FFE:]
    slope = (2.0 / 3.141592653589793) ** 0.5
    bend = jnp.tanh(slope * (lower + 0.044715 * lower * lower * lower))
    gelu = 0.5 * lower * (1.0 + bend)
    gelu_grad = 0.5 * (1.0 + bend) + 0.5 * lower * (1.0 - bend * bend) * slope * (
        1.0 + 3 * 0.044715 * lower * lower
    )
    inner = (gelu * upper).astype(bf16)
    inner_ref[...] = inner
    out = dot(inner, down_ref[...]).astype(bf16)
    out_ref[...] = out
    grad = grad_ref[:, :width].astype(f32)
    d_gate = jnp.sum(out.astype(f32) * grad, axis=-1, keepdims=True)
    d_gate_high = d_gate.astype(bf16).astype(f32)
    column = lax.broadcasted_iota(jnp.int32, (rows.shape[0], EXTRA), 1)
    d_in_ref[:, width:] = jnp.where(
        column == expert_ref[1],
        d_gate_high,
        jnp.where(column == expert_ref[1] + EXPERTS // 2, d_gate - d_gate_high, 0.0),
    ).astype(bf16)
    d_out = (gate * grad).astype(bf16)
    d_out_ref[...] = d_out
    d_inner = dot_t(d_out, down_ref[...])
    d_projected_ref[:, :FFE] = (d_inner * upper * gelu_grad).astype(bf16)
    d_projected_ref[:, FFE:] = (d_inner * gelu).astype(bf16)
    d_in_ref[:, :width] = dot_t(d_projected_ref[...], up_ref[...]).astype(bf16)


def expert_part(expert, received, grad_rows, router, up, down):
    rows, model_width = received.shape
    block = 256

    def row_block(width):
        return pl.BlockSpec((block, width), lambda i, *_: (i, 0))

    def whole(array):
        return pl.BlockSpec(array.shape, lambda i, *_: (0, 0))

    widths = (FFE, model_width, model_width, 2 * FFE, model_width + EXTRA)
    return pl.pallas_call(
        expert_kernel,
        grid_spec=pltpu.PrefetchScalarGridSpec(
            num_scalar_prefetch=1,
            grid=(rows // block,),
            in_specs=[
                row_block(model_width),
                row_block(model_width + EXTRA),
                whole(router),
                whole(up),
                whole(down),
            ],
            out_specs=[row_block(width) for width in widths],
        ),
        out_shape=[jax.ShapeDtypeStruct((rows, width), bf16) for width in widths],
        compiler_params=pltpu.CompilerParams(vmem_limit_bytes=VMEM_LIMIT),
        cost_estimate=pl.CostEstimate(flops=0, bytes_accessed=0, transcendentals=0),
    )(expert, received, grad_rows, router, up, down)


def token_backward_kernel(
    core_ref,
    place_ref,
    back_ref,
    far_ref,
    spread_ref,
    gates_ref,
    router_ref,
    xn_ref,
    hidden_ref,
    gain_ref,
    grad_ref,
    weight_ref,
    d_hidden_ref,
    d_hidden_b_ref,
    d_attended_ref,
    small_ref,
):
    width = hidden_ref.shape[1]
    part = EXPERTS // 2
    wide = t_dot(place_ref[...], back_ref[...])
    far = far_ref[...]
    d_gates = jnp.zeros(gates_ref.shape, f32)
    for number, extra in enumerate((wide[:, width:].astype(bf16), far[:, width:])):
        for start in (0, part):
            d_gates = d_gates + dot(extra[:, start : start + part], spread_ref[number])
    gates = gates_ref[...]
    d_chosen = gates * (d_gates - jnp.sum(gates * d_gates, axis=-1, keepdims=True))
    d_logits = d_chosen.astype(bf16)
    d_xn = dot_t(d_logits, router_ref[...]) + wide[:, :width] + far[:, :width].astype(f32)
    hidden = hidden_ref[...]
    scale = lax.rsqrt(jnp.mean(hidden * hidden, axis=-1, keepdims=True) + EPSILON)
    normed = hidden * scale
    scaled = d_xn * gain_ref[...]
    d_hidden = grad_ref[...].astype(f32) + scale * (
        scaled - normed * jnp.mean(scaled * normed, axis=-1, keepdims=True)
    )
    d_hidden_ref[...] = d_hidden
    d_hidden_b = d_hidden.astype(bf16)
    d_hidden_b_ref[...] = d_hidden_b
    small_ref[:EXPERTS] = t_dot(d_logits, xn_ref[...])
    small_ref[EXPERTS:] = jnp.broadcast_to(jnp.sum(d_xn * normed, axis=0, keepdims=True), (8, width))
    d_attended = dot_t(d_hidden_b, weight_ref[...]).astype(bf16)
    first, last = d_attended[:, : width // 2], d_attended[:, width // 2 :]
    lower = core_ref[0] == 0
    d_attended_ref[0] = jnp.where(lower, first, last)
    d_attended_ref[1] = jnp.where(lower, last, first)


def token_backward(core, place, back, far, spread, gates, router, xn, hidden, gain, grad, weight):
    seq_len, width = hidden.shape
    return pl.pallas_call(
        token_backward_kernel,
        in_specs=[pl.BlockSpec(memory_space=pltpu.SMEM)] + [pl.BlockSpec(memory_space=pltpu.VMEM)] * 11,
        out_specs=[pl.BlockSpec(memory_space=pltpu.VMEM)] * 4,
        out_shape=[
            jax.ShapeDtypeStruct((seq_len, width), f32),
            jax.ShapeDtypeStruct((seq_len, width), bf16),
            jax.ShapeDtypeStruct((2, seq_len, width // 2), bf16),
            jax.ShapeDtypeStruct((EXPERTS + 8, width), f32),
        ],
        compiler_params=pltpu.CompilerParams(vmem_limit_bytes=VMEM_LIMIT),
        cost_estimate=pl.CostEstimate(flops=0, bytes_accessed=0, transcendentals=0),
    )(core, place, back, far, spread, gates, router, xn, hidden, gain, grad, weight)


def expert_weights_kernel(x_own, x_far, p_own, p_far, i_own, i_far, d_own, d_far, up_ref, down_ref):
    up_ref[...] = (t_dot(x_own[...], p_own[...]) + t_dot(x_far[...], p_far[...])).astype(bf16)
    down_ref[...] = (t_dot(i_own[...], d_own[...]) + t_dot(i_far[...], d_far[...])).astype(bf16)


def expert_weights(received, d_projected, inner, d_out):
    rows, model_width = received[0].shape
    steps = 3

    def columns(array):
        return pl.BlockSpec((rows, array.shape[1] // steps), lambda i: (0, i))

    def whole(array):
        return pl.BlockSpec(array.shape, lambda i: (0, 0))

    return pl.pallas_call(
        expert_weights_kernel,
        grid=(steps,),
        in_specs=[columns(a) for a in received]
        + [whole(a) for a in d_projected]
        + [columns(a) for a in inner]
        + [whole(a) for a in d_out],
        out_specs=[
            pl.BlockSpec((model_width // steps, 2 * FFE), lambda i: (i, 0)),
            pl.BlockSpec((FFE // steps, model_width), lambda i: (i, 0)),
        ],
        out_shape=[
            jax.ShapeDtypeStruct((model_width, 2 * FFE), bf16),
            jax.ShapeDtypeStruct((FFE, model_width), bf16),
        ],
        compiler_params=pltpu.CompilerParams(vmem_limit_bytes=VMEM_LIMIT),
        cost_estimate=pl.CostEstimate(flops=0, bytes_accessed=0, transcendentals=0),
    )(*received, *d_projected, *inner, *d_out)


def shards(
    tokens,
    routes,
    norm_attn,
    qkv_weight,
    out_weight,
    norm_moe,
    router_weight,
    gate_up,
    down,
    grad_output,
):
    seq_len, model_width = tokens.shape
    query_half = HEADS * HEAD_DIM // 2
    kv_half = KV_HEADS * HEAD_DIM // 2
    out_half = out_weight.shape[1] // 2
    groups = lax.axis_size(EXPERT)
    fsdp = lax.axis_size(FSDP)
    half_devices = groups * fsdp // 2
    local_count = gate_up.shape[0]
    parts = fsdp // local_count
    half_experts = EXPERTS // 2
    rows = half_experts * CAP
    core = lax.axis_index("c")
    half = lax.axis_index("h")
    me = lax.axis_index(FSDP)
    group = lax.axis_index(EXPERT)
    my_expert = jnp.stack(
        [
            group * local_count + me // parts,
            group * (local_count // 2) + me // parts - half * (local_count // 2),
        ]
    ).astype(jnp.int32)

    box = {}

    def tie(value, *names):
        value, held = together(value, [box[name] for name in names])
        box.update(zip(names, held))
        return value

    up_width, down_width = gate_up.shape[1], down.shape[1]
    columns = fsdp // 4

    def target(index, move, sign=1):
        step, cross = move
        line = index // columns
        line = (line + sign * step + 4) % 4 if step >= 0 else line ^ -step
        return line * columns + (index % columns ^ cross)

    def every(moves):
        return [
            (step, other) for step, cross in moves for other in (range(1, columns) if cross else range(1))
        ]

    def fetch(moves, *names):
        for move in every(moves):
            expert = target(me, move) // parts
            piece = jnp.concatenate(
                [
                    lax.dynamic_index_in_dim(gate_up, expert, 0, keepdims=False),
                    lax.dynamic_index_in_dim(down, expert, 0, keepdims=False),
                ],
                axis=0,
            )
            if move != (0, 0):
                piece = lax.ppermute(tie(piece, *names), FSDP, [(i, target(i, move)) for i in range(fsdp)])
            box["in", move] = piece

    def coming(moves):
        return [("in", move) for move in every(moves)]

    def assemble():
        up_full = jnp.zeros((fsdp * up_width, gate_up.shape[2]), gate_up.dtype)
        down_full = jnp.zeros((fsdp * down_width, down.shape[2]), down.dtype)
        for move in every(sum(INWARD, [(0, 0)])):
            source, piece = target(me, move, -1), box["in", move]
            up_full = lax.dynamic_update_slice(up_full, piece[:up_width], (source * up_width, 0))
            down_full = lax.dynamic_update_slice(down_full, piece[up_width:], (source * down_width, 0))
        return up_full, down_full

    def give(moves, up_grad, down_grad, *names):
        for move in every(moves):
            to = target(me, move)
            piece = jnp.concatenate(
                [
                    lax.dynamic_slice_in_dim(up_grad, to * up_width, up_width, axis=0),
                    lax.dynamic_slice_in_dim(down_grad, to * down_width, down_width, axis=0),
                ],
                axis=0,
            )
            if move != (0, 0):
                piece = lax.ppermute(tie(piece, *names), FSDP, [(i, target(i, move)) for i in range(fsdp)])
            box["out", move] = piece

    def going(moves):
        return [("out", move) for move in every(moves)]

    def collect():
        up_sum = jnp.zeros(gate_up.shape, f32)
        down_sum = jnp.zeros(down.shape, f32)
        for move in every(sum(OUTWARD, [(0, 0)])):
            expert = target(me, move, -1) // parts
            piece = box["out", move].astype(f32)[None]
            up_part, down_part = piece[:, :up_width], piece[:, up_width:]
            if parts > 1:
                up_part = up_part + lax.dynamic_slice_in_dim(up_sum, expert, 1, axis=0)
                down_part = down_part + lax.dynamic_slice_in_dim(down_sum, expert, 1, axis=0)
            up_sum = lax.dynamic_update_slice(up_sum, up_part, (expert, 0, 0))
            down_sum = lax.dynamic_update_slice(down_sum, down_part, (expert, 0, 0))
        return up_sum, down_sum

    def exchange(buffer):
        shape = buffer.shape
        return lax.all_to_all(
            buffer.reshape((half_devices, rows // half_devices) + shape[1:]),
            HALF,
            split_axis=0,
            concat_axis=0,
            tiled=True,
        ).reshape(shape)

    def half_columns(table, index):
        cube = table.reshape(table.shape[0], groups, 2, local_count // 2)
        return lax.dynamic_index_in_dim(cube, index, 2, keepdims=False).reshape(table.shape[0], half_experts)

    token_f = tokens.astype(f32)

    qkv_mine = jnp.concatenate(
        [
            lax.dynamic_slice_in_dim(qkv_weight, core * query_half, query_half, axis=1),
            lax.dynamic_slice_in_dim(qkv_weight, 2 * query_half + core * kv_half, kv_half, axis=1),
            lax.dynamic_slice_in_dim(qkv_weight, 2 * query_half + (2 + core) * kv_half, kv_half, axis=1),
        ],
        axis=1,
    )
    out_mine = lax.dynamic_slice_in_dim(out_weight, core * out_half, out_half, axis=1)
    expert_ids = jnp.arange(EXPERTS, dtype=jnp.int32)
    order = jnp.arange(seq_len)
    earlier = (order[None, :] < order[:, None]).astype(bf16)

    def placing(routing):
        mask = jnp.any(routing[:, :, None] == expert_ids[None, None, :], axis=1)
        position = dot(earlier, mask.astype(bf16)).astype(jnp.int32)
        slot = half_columns(jnp.where(mask, position, -1), half).T
        place = slot[:, None, :] == jnp.arange(CAP, dtype=jnp.int32)[None, :, None]
        return mask, place

    mask_own, cube_own = placing(routes)
    mask_far, cube_far = placing(swap(routes, "h"))
    place_own = cube_own.astype(bf16).reshape(rows, seq_len)
    place_far = cube_far.astype(bf16).reshape(rows, seq_len)

    def first_done(block):
        nonlocal gate_up, down
        sent, block, gate_up, down = together(grad_output, block, gate_up, down)
        box["grad_far"] = swap(sent, "h")
        fetch(INWARD[0])
        return mark(block)

    def send_rows(place, grad, mask):
        extra = jnp.pad(mask.astype(bf16), ((0, 0), (0, EXTRA - EXPERTS)))
        return dot(place, jnp.concatenate([grad, extra], axis=1)).astype(bf16)

    xn_first_f, norm_first_pull = jax.vjp(rms_apply, token_f, norm_attn)
    xn_first = xn_first_f.astype(bf16)
    xn_pair = jnp.concatenate([xn_first, swap(xn_first, "c")], axis=0)
    shard = jnp.concatenate([qkv_mine, out_mine], axis=1)
    core_weights, xn_pair, own_sent = tie(
        (gather_shards(shard, first_done), xn_pair, send_rows(place_own, grad_output, mask_own)),
        "grad_far",
        *coming(INWARD[0]),
    )
    fetch(INWARD[1], *coming(INWARD[0]))
    box["grad_rows_own"] = exchange(own_sent)
    xn_pair = mark(xn_pair)
    qkv_width = query_half + 2 * kv_half
    qkv_core, out_core = core_weights[:, :qkv_width], core_weights[:, qkv_width:]

    joint, attended_mine = attend(xn_pair, qkv_core, seq_len)
    out_full = order_by(core, out_core, swap(out_core, "c"), 1)
    attended_mine = attended_mine.reshape(2, seq_len, query_half)
    far_sent = send_rows(place_far, box["grad_far"], mask_far)
    attended_mine, far_sent = tie((attended_mine, far_sent), "grad_rows_own", *coming(INWARD[1]))
    fetch(INWARD[2], *coming(INWARD[1]))
    box["grad_rows_far"] = exchange(far_sent)
    attended_mine = mark(attended_mine)
    attended_other = swap(attended_mine, "c")
    attended = order_by(core, attended_mine[0], attended_other[1], 1)
    attended_next = order_by(core, attended_mine[1], attended_other[0], 1)
    hidden = token_f + dot(attended, out_full)
    xn_second = rms_apply(hidden, norm_moe).astype(bf16)

    def gating(values_b, mask):
        logits = dot(values_b, router_weight)
        top = jnp.max(jnp.where(mask, logits, -1e30), axis=-1, keepdims=True)
        exponent = jnp.where(mask, jnp.exp(jnp.where(mask, logits - top, 0.0)), 0.0)
        total = jnp.sum(exponent, axis=-1, keepdims=True)
        return exponent / jnp.where(total > 0, total, 1.0)

    own_sent, xn_sent = tie(
        (dot(place_own, xn_second).astype(bf16), xn_second), "grad_rows_far", *coming(INWARD[2])
    )
    fetch(INWARD[3], *coming(INWARD[2]))
    box["received_own"] = exchange(mark(own_sent))
    fetch([(0, 0)])
    box["in", (0, 0)] = mark(tie(box["in", (0, 0)], *coming(INWARD[2])))
    xn_sent = tie(xn_sent, "received_own", *coming(INWARD[3]))
    box["xn_far"] = swap(xn_sent, "h")
    fetch(INWARD[4], *coming(INWARD[3]))
    far_sent = tie(dot(place_far, box["xn_far"]).astype(bf16), *coming(INWARD[4]))
    box["received_far"] = exchange(far_sent)
    gate_up_full, down_full = assemble()
    box["own"] = expert_part(
        my_expert, box["received_own"], box["grad_rows_own"], router_weight, gate_up_full, down_full
    )
    xn_far = box["xn_far"]
    gates = gating(xn_second, mask_own)
    gates_far = gating(xn_far, mask_far)

    box["back_in_own"] = exchange(tie(box["own"][4], "received_far"))
    box["far"] = expert_part(
        my_expert, box["received_far"], box["grad_rows_far"], router_weight, gate_up_full, down_full
    )
    received, d_projected, inner, d_out = [
        list(pair)
        for pair in zip(
            (box["received_own"], box["own"][3], box["own"][0], box["own"][2]),
            (box["received_far"], box["far"][3], box["far"][0], box["far"][2]),
        )
    ]
    up_grad, down_grad = expert_weights(received, d_projected, inner, d_out)
    sent, up_grad, down_grad = tie((box["far"][4], up_grad, down_grad), "back_in_own")
    box["back_in_far"] = exchange(sent)
    give(OUTWARD[0], up_grad, down_grad)
    box["d_in_sum_far"] = swap(t_dot(place_far, box["back_in_far"]).astype(bf16), "h")
    give([(0, 0)], up_grad, down_grad)

    places = jnp.arange(EXPERTS) // local_count * (local_count // 2) + jnp.arange(EXPERTS) % (local_count // 2)
    side = jnp.arange(EXPERTS) % local_count // (local_count // 2)
    mine = (places[None, :] == jnp.arange(half_experts)[:, None]).astype(bf16)
    spread = jnp.stack([mine * (side == half), mine * (side != half)]).astype(bf16)
    d_hidden, d_hidden_b, d_attended, router_moe = token_backward(
        core.reshape(1).astype(jnp.int32),
        place_own,
        box["back_in_own"],
        box["d_in_sum_far"],
        spread,
        gates,
        router_weight,
        xn_second,
        hidden,
        norm_moe[None],
        grad_output,
        out_full,
    )

    def mix(cube, gate, back):
        spread = jnp.where(cube, half_columns(gate, half).T[:, None, :], 0.0).reshape(rows, seq_len)
        high = spread.astype(bf16)
        low = (spread - high.astype(f32)).astype(bf16)
        return t_dot(high, back) + t_dot(low, back)

    d_hidden_b, up_grad, down_grad, out_far = together(d_hidden_b, up_grad, down_grad, box["far"][1])
    give(OUTWARD[1], up_grad, down_grad)
    box["back_out_far"] = exchange(mark(out_far))

    def halves(value):
        first, last = jnp.split(value, 2, axis=1)
        return jnp.where(core == 0, first, last), jnp.where(core == 0, last, first)

    grad_heads = jnp.stack([d_attended[0], swap(d_attended[1], "c")]).reshape(2 * seq_len, query_half)
    d_hid_mine, d_hid_send = halves(d_hidden_b)
    d_hid_next = swap(d_hid_send, "c")
    out_pair = (
        jnp.concatenate([attended, attended_next], axis=0),
        jnp.concatenate([d_hid_mine, d_hid_next], axis=0),
    )
    out_sends = scatter_sends(*out_pair)
    grad_heads = mark(grad_heads)
    grad_joint, d_xn_pair = attend_backward(joint, grad_heads, qkv_core, seq_len)
    grad_joint, out_own = tie((grad_joint, box["own"][1]), "back_out_far")
    box["back_out_own"] = exchange(out_own)
    moe_sent = mix(cube_far, gates_far, box["back_out_far"]).astype(bf16)

    def first_round(blocks):
        blocks, sent, box["small"] = tie((blocks, moe_sent, box["small"]), *going(OUTWARD[0] + OUTWARD[1]))
        give(OUTWARD[2], up_grad, down_grad)
        box["moe_far"] = swap(sent, "h")
        box["small"] = sum_over(box["small"], ("c", "y", "r", "h"))
        return blocks

    def second_round(blocks):
        blocks = tie(blocks, "moe_far", *going(OUTWARD[2]))
        give(OUTWARD[3], up_grad, down_grad, *going(OUTWARD[2]))
        return blocks

    def third_round(blocks):
        return tie(blocks, *going(OUTWARD[3]))

    d_xn_first = d_xn_pair[:seq_len] + swap(d_xn_pair[seq_len:], "c")
    d_token_norm, gain_attn_local = norm_first_pull(d_xn_first)
    grad_tokens = d_hidden + d_token_norm

    box["small"] = jnp.concatenate([router_moe[: EXPERTS + 1], gain_attn_local[None]], axis=0)
    qkv_grad, out_grad = scatter_products(
        ((xn_pair, grad_joint), out_pair),
        (scatter_sends(xn_pair, grad_joint), out_sends),
        (first_round, second_round, third_round),
    )
    moe_own = mix(cube_own, gates, box["back_out_own"])
    small = box["small"]
    mixed = (hidden + (moe_own + box["moe_far"].astype(f32))).astype(bf16)
    grad_gate_up, grad_down = collect()
    grad_out_proj = order_by(core, out_grad.astype(f32), swap(out_grad, "c").astype(f32), 1)
    qkv_grad_other = swap(qkv_grad, "c")
    first = jnp.where(core == 0, qkv_grad, qkv_grad_other).astype(f32)
    last = jnp.where(core == 0, qkv_grad_other, qkv_grad).astype(f32)
    cut = (query_half, query_half + kv_half)
    grad_qkv = jnp.concatenate(
        [piece for pair in zip(jnp.split(first, cut, axis=1), jnp.split(last, cut, axis=1)) for piece in pair],
        axis=1,
    )

    return (
        mixed,
        grad_tokens,
        small[EXPERTS + 1],
        grad_qkv,
        grad_out_proj,
        small[EXPERTS],
        small[:EXPERTS].T,
        grad_gate_up,
        grad_down,
    )


def solution(mesh):
    expert, fsdp = mesh.devices.shape
    fine = Mesh(mesh.devices.reshape(expert // 2, 2, 2, fsdp // 2), BOTH)
    in_specs = (
        P(BOTH, None),
        P(BOTH, None),
        P(),
        P(FSDP, None),
        P(FSDP, None),
        P(),
        P(),
        P(EXPERT, FSDP, None),
        P(EXPERT, FSDP, None),
        P(BOTH, None),
    )
    out_specs = (
        P(BOTH, None),
        P(BOTH, None),
        P(),
        P(FSDP, None),
        P(FSDP, None),
        P(),
        P(),
        P(EXPERT, FSDP, None),
        P(EXPERT, FSDP, None),
    )
    return jax.shard_map(shards, mesh=fine, in_specs=in_specs, out_specs=out_specs, check_vma=False)
```
